512 devices in a mesh: expert: 32 (over y, x, core), dp: 16 (over z).
Axes of the slice: x: 4, y: 4, z: 16, core: 2. Of those that a mesh axis runs over, the one named last changes fastest.
Arguments:
- tokens: bfloat16 [4096, 7168], P('expert', 'dp'), may hold values from -6 to 6
- routes: int32 [4096, 2], P('expert'), may hold values from 0 to 15, all different within a row; in each aligned block of 128 rows (0 to 127, 128 to 255, ...) at most 32 rows name the same one
- route_weight: float32 [4096, 2], P('expert'), may hold values from 0.1 to 1
- w_gate: bfloat16 [7168, 16384], P('dp', 'expert'), may hold values from -0.0625 to 0.0625
- w_up: bfloat16 [7168, 16384], P('dp', 'expert'), may hold values from -0.0625 to 0.0625
- w_down: bfloat16 [16384, 7168], P('expert', 'dp'), may hold values from -0.1875 to 0.1875
- cotangent: bfloat16 [4096, 7168], P('expert', 'dp'), may hold values from -1.1953125 to 1.1953125
Outputs:
- output: bfloat16 [4096, 7168], P('expert', 'dp')
- grad_tokens: bfloat16 [4096, 7168], P('expert', 'dp')
- grad_gate: bfloat16 [7168, 16384], P('dp', 'expert')
- grad_up: bfloat16 [7168, 16384], P('dp', 'expert')
- grad_down: bfloat16 [16384, 7168], P('expert', 'dp')
The draws below stay inside these ranges and needn't reach their ends.
Inputs may be any that keep to these rules, and one draw needn't show every extreme that they name: `routes`: each token names 2 different experts. Among the 128 tokens of one index of expert no expert is named more than 32 times, and in every draw some expert is named exactly 32 times by the tokens of some index.
All inputs are finite; a program needn't handle non-finite values.
Results may differ from the reference program's by a relative error of at most 0.035.
Values may be sent and summed in bfloat16 or wider, within the bound.
No kernel may reach another device: no remote copies, remote signals or barrier semaphores. Data moves between devices by JAX's collectives and lax.ppermute only.
A program may use at most 64 MiB of HBM per device.

```python
import math
import jax
import jax.numpy as jnp
import numpy as np
from jax import lax

D = 7168
FF = 1024
TOP = 2
TOK_DEV = 128
HALF = 512
EXPERTS = 16
CAP = 32
DSL = 448
TOKENS = 4096
N_EXPERT = 32
N_DP = 16


def block_levels(rng, shape, pieces, low, top_value):
    factor_of, own = 1.0, jax.random.fold_in(rng, 6)
    for axis_at, blocks in pieces:
        steps = jnp.exp(jax.random.uniform(jax.random.fold_in(own, axis_at), (blocks,), jnp.float32, low / len(pieces), top_value / len(pieces)))
        factor_of = factor_of * jnp.repeat(steps, shape[axis_at] // blocks).reshape([-1 if axis == axis_at else 1 for axis in range(len(shape))])
    return factor_of


def assign_block(rng, own, number, rows, amount, top, limit, lean):
    order = jax.random.permutation(rng, amount)
    heavy_load, usual = load_shares(amount, rows * top, limit, lean, True), load_shares(amount, rows * top, limit, lean, False)
    places = jnp.arange(amount)

    def named(tallies, offset_by):
        used = int((tallies > 0).sum())
        fixed = max(1, used // 4)
        moved = fixed + (places - fixed + offset_by * (used - fixed)) % max(1, amount - fixed)
        return jnp.zeros((amount,), jnp.int32).at[order[jnp.where(places < fixed, places, moved)]].set(jnp.asarray(tallies, jnp.int32))

    tallies = jnp.where(number % 4 == 0, named(heavy_load, number // 4), named(usual, number - number // 4 - 1))
    mixed = jax.random.permutation(jax.random.fold_in(own, 3), amount)
    source_of, sink = mixed[0:amount // 2 * 2:2], mixed[1:amount // 2 * 2:2]
    margin = jnp.minimum(tallies[source_of] - 1, limit - tallies[sink]) // 2
    margin = jnp.where((source_of == order[0]) | (sink == order[0]) | (tallies[sink] == 0), 0, jnp.maximum(margin, 0))
    moved = jax.random.randint(jax.random.fold_in(own, 4), (amount // 2,), 0, 1 << 20) % (margin + 1)
    tallies = tallies.at[source_of].add(-moved).at[sink].add(moved)
    items = jnp.searchsorted(jnp.cumsum(tallies), jnp.arange(rows * top), side="right").astype(jnp.int32)
    table = items.reshape(top, rows).T
    table = table[jax.random.permutation(jax.random.fold_in(own, 1), rows)]
    offset_by = jax.random.randint(jax.random.fold_in(own, 2), (rows, 1), 0, top)
    return jnp.take_along_axis(table, (jnp.arange(top)[None, :] + offset_by) % top, axis=1)


def load_shares(count, total, bound, skew, full):
    portions = [(1 << 20) // math.isqrt(grade ** skew) + 1 for grade in range(1, count + 1)]
    largest = bound if full else min(bound, max(-(-total // count), total * portions[0] // sum(portions)))
    least = 1 if total - largest >= count - 1 else 0
    holding, surplus = [largest] + [least] * (count - 1), total - largest - least * (count - 1)
    while surplus > 0:
        candidates = [i for i in range(1, count) if holding[i] < largest] or [i for i in range(1, count) if holding[i] < bound]
        mass, left = sum([portions[i] for i in candidates]), surplus
        for i in candidates:
            addition = min(bound - holding[i], max(1, left * portions[i] // mass), surplus)
            holding[i] = holding[i] + addition
            surplus = surplus - addition
    return np.array(holding)


def noise(rng, dims, scale, limit, shards=(), kind=jnp.bfloat16):
    level = block_levels(rng, dims, shards, -0.22, 0.18) if shards else 1.0
    result = jax.random.normal(rng, dims, jnp.float32) * scale * level
    return jnp.minimum(jnp.maximum(result, -limit), limit).astype(kind)


def setup_inputs(seed: int = 0) -> dict:
    arg_keys = jax.random.split(jax.random.key(seed), 8)
    tokens = noise(arg_keys[0], (TOKENS, D), 1.0, 6.0, ((0, 32), (1, 16)))
    routes_keys = jax.random.split(jax.random.fold_in(arg_keys[1], 1), TOKENS // TOK_DEV)
    routes_turns = jax.random.permutation(jax.random.fold_in(arg_keys[1], 3), TOKENS // TOK_DEV)
    routes = jax.vmap(lambda own, number: assign_block(jax.random.fold_in(arg_keys[1], 2), own, number, TOK_DEV, EXPERTS, TOP, CAP, 2))(routes_keys, routes_turns).reshape((TOKENS, TOP))
    route_weight = jnp.clip(0.1 + 0.9 * jax.random.uniform(arg_keys[2], (TOKENS, TOP), jnp.float32) ** block_levels(arg_keys[2], (TOKENS, TOP), ((0, 32),), -0.2, 0.2), 0.1, 1.0)
    w_gate = noise(arg_keys[3], (D, EXPERTS * FF), D ** -0.5, 0.0625, ((0, 16), (1, 32)))
    w_up = noise(arg_keys[4], (D, EXPERTS * FF), D ** -0.5, 0.0625, ((0, 16), (1, 32)))
    w_down = noise(arg_keys[5], (EXPERTS * FF, D), FF ** -0.5, 0.1875, ((0, 32), (1, 16)))
    cotangent = noise(arg_keys[6], (TOKENS, D), 0.2, 1.1953125, ((0, 32), (1, 16)))
    return dict(tokens=tokens, routes=routes, route_weight=route_weight, w_gate=w_gate, w_up=w_up, w_down=w_down, cotangent=cotangent)


def block_sums(left, right):
    rows = left.shape[0]
    parts = jnp.einsum("tjd,jdf->jtf", left.astype(jnp.float32).reshape(rows, N_DP, DSL),
                       right.astype(jnp.float32).reshape(N_DP, DSL, right.shape[1]),
                       precision=lax.Precision.HIGHEST)
    rounded = lax.optimization_barrier(parts.astype(jnp.bfloat16))
    return jnp.sum(rounded.astype(jnp.float32), axis=0)


def reference(tokens, routes, route_weight, w_gate, w_up, w_down, cotangent):
    cot_wide = cotangent.astype(jnp.float32)
    tok_wide = tokens.astype(jnp.float32)
    slots_all = N_EXPERT * CAP

    def one_expert(carry, expert):
        out_acc, back_acc = carry
        hits = (routes == expert).astype(jnp.float32)
        mask = jnp.sum(hits, axis=1)
        weight = jnp.sum(hits * route_weight, axis=1)
        picked = jnp.nonzero(mask > 0.5, size=slots_all, fill_value=0)[0].astype(jnp.int32)
        in_range = (jnp.arange(slots_all, dtype=jnp.int32).astype(mask.dtype) < jnp.sum(mask)).astype(mask.dtype)
        valid = mask[picked] * in_range
        chosen_w = weight[picked] * in_range
        gate_cols = lax.dynamic_slice_in_dim(w_gate, expert * FF, FF, 1)
        up_cols = lax.dynamic_slice_in_dim(w_up, expert * FF, FF, 1)
        down_rows = lax.dynamic_slice_in_dim(w_down, expert * FF, FF, 0)
        inputs = (tok_wide[picked] * valid[:, None]).astype(jnp.bfloat16)
        scaled = (chosen_w[:, None] * cot_wide[picked]).astype(jnp.bfloat16)
        gate_pre = block_sums(inputs, gate_cols)
        up_pre = block_sums(inputs, up_cols)
        down_back = block_sums(scaled, down_rows.T)
        sig = jax.nn.sigmoid(gate_pre)
        active = gate_pre * sig
        hidden = (active * up_pre).astype(jnp.bfloat16)
        grad_gp = (down_back * up_pre * sig * (1.0 + gate_pre * (1.0 - sig))).astype(jnp.bfloat16)
        grad_up = (down_back * active).astype(jnp.bfloat16)
        out_halves = []
        back_halves = []
        for half_index in range(2):
            lo = half_index * HALF
            out_halves.append(jnp.dot(hidden[:, lo:lo + HALF], down_rows[lo:lo + HALF],
                                      preferred_element_type=jnp.float32).astype(jnp.bfloat16))
            back = jnp.dot(grad_gp[:, lo:lo + HALF], gate_cols[:, lo:lo + HALF].T, preferred_element_type=jnp.float32)
            back = back + jnp.dot(grad_up[:, lo:lo + HALF], up_cols[:, lo:lo + HALF].T, preferred_element_type=jnp.float32)
            back_halves.append(back.astype(jnp.bfloat16))
        expert_out = (out_halves[0].astype(jnp.float32) + out_halves[1].astype(jnp.float32)).astype(jnp.bfloat16)
        expert_back = (back_halves[0].astype(jnp.float32) + back_halves[1].astype(jnp.float32)).astype(jnp.bfloat16)
        out_acc = out_acc.at[picked].add(chosen_w[:, None] * expert_out.astype(jnp.float32))
        back_acc = back_acc.at[picked].add(valid[:, None] * expert_back.astype(jnp.float32))
        grad_g = jnp.dot(inputs.T, grad_gp, preferred_element_type=jnp.float32).astype(jnp.bfloat16)
        grad_u = jnp.dot(inputs.T, grad_up, preferred_element_type=jnp.float32).astype(jnp.bfloat16)
        grad_d = jnp.dot(hidden.T, scaled, preferred_element_type=jnp.float32).astype(jnp.bfloat16)
        return (out_acc, back_acc), (grad_g, grad_u, grad_d)

    zeros = jnp.zeros(tokens.shape, jnp.float32)
    (out_acc, back_acc), stacked = lax.scan(one_expert, (zeros, zeros), jnp.arange(EXPERTS, dtype=jnp.int32))
    grad_g, grad_u, grad_d = stacked
    grad_gate = jnp.transpose(grad_g, (1, 0, 2)).reshape(D, EXPERTS * FF)
    grad_up_all = jnp.transpose(grad_u, (1, 0, 2)).reshape(D, EXPERTS * FF)
    grad_down = grad_d.reshape(EXPERTS * FF, D)
    return (out_acc.astype(jnp.bfloat16), back_acc.astype(jnp.bfloat16), grad_gate, grad_up_all, grad_down)
```

```python
import functools

import jax
import jax.numpy as jnp
from jax import lax
from jax.experimental import pallas as pl
from jax.experimental.pallas import tpu as pltpu
from jax.sharding import PartitionSpec as P

BF = jnp.bfloat16
F32 = jnp.float32
VMEM_BYTES = 48 * 1024 * 1024


def dot_nn(a, b):
    return lax.dot_general(a, b, (((1,), (0,)), ((), ())), preferred_element_type=F32)


def dot_nt(a, b):
    return lax.dot_general(a, b, (((1,), (1,)), ((), ())), preferred_element_type=F32)


def dot_tn(a, b):
    return lax.dot_general(a, b, (((0,), (0,)), ((), ())), preferred_element_type=F32)


def params(**more):
    return pltpu.CompilerParams(vmem_limit_bytes=VMEM_BYTES, **more)


def cost(flops, moved):
    return pl.CostEstimate(flops=flops, bytes_accessed=moved, transcendentals=0)


def pickers(routes, experts, cap):
    top, ntok = routes.shape
    names = lax.broadcasted_iota(jnp.int32, (experts, ntok), 0)
    hits = [routes[k : k + 1, :] == names for k in range(top)]
    mask = sum(jnp.where(h, 1.0, 0.0) for h in hits)
    before = lax.broadcasted_iota(jnp.int32, (ntok, ntok), 0) < lax.broadcasted_iota(
        jnp.int32, (ntok, ntok), 1
    )
    slot = dot_nn(mask.astype(BF), jnp.where(before, 1.0, 0.0).astype(BF))
    want = lax.broadcasted_iota(jnp.int32, (experts, cap, ntok), 1).astype(F32)
    picks = []
    for h in hits:
        own = jnp.where(h, slot, -1.0)
        own = jnp.broadcast_to(own[:, None, :], (experts, cap, ntok))
        pick = jnp.where(own == want, 1.0, 0.0)
        picks.append(pick.reshape(experts * cap, ntok).astype(BF))
    return picks


def send_kernel(experts, cap, tok_ref, cot_ref, routes_ref, weight_ref, out_ref):
    dsl, ntok = tok_ref.shape
    picks = pickers(routes_ref[...], experts, cap)
    x = dot_nt(picks[0] + picks[1], tok_ref[...]).astype(BF)
    out_ref[:, :cap, :] = x.reshape(experts, cap, dsl)
    cot = cot_ref[...].astype(F32)
    weight = weight_ref[...]
    dy = sum(
        dot_nt(picks[k], (cot * weight[k : k + 1, :]).astype(BF)) for k in range(2)
    ).astype(BF)
    out_ref[:, cap:, :] = dy.reshape(experts, cap, dsl)


def terms_kernel(cap, rows_ref, wg_ref, wu_ref, wd_ref, *rest):
    sources, _, dsl = rows_ref.shape
    outs, (held, sems) = rest[:-2], rest[-2:]
    half = wg_ref.shape[1]
    step = 256 // cap
    copies = []
    for lo in range(0, sources, step):
        x = rows_ref[lo : lo + step, :cap, :].reshape(step * cap, dsl)
        dy = rows_ref[lo : lo + step, cap:, :].reshape(step * cap, dsl)
        at = slice(lo * cap, (lo + step) * cap)
        for j, (left, w_ref) in enumerate(((x, wg_ref), (x, wu_ref), (dy, wd_ref))):
            held[at, j * half : (j + 1) * half] = dot_nn(left, w_ref[...]).astype(BF)
            for i in range(lo, lo + step):
                k = 3 * i + j
                copies.append(
                    pltpu.make_async_copy(
                        held.at[pl.ds(i * cap, cap), pl.ds(j * half, half)],
                        outs[k],
                        sems.at[k],
                    )
                )
                copies[-1].start()
    for c in copies:
        c.wait()


def back_kernel(cap, n, *refs):
    pieces, (wg_ref, wu_ref, wd_ref, acts_ref, ret_ref, held, sems) = refs[:n], refs[n:]
    sources = n // 3
    half = wg_ref.shape[1]
    dsl = wg_ref.shape[0]

    def copy(k):
        i, j = divmod(k, 3)
        return pltpu.make_async_copy(
            pieces[k],
            held.at[pl.ds(i * cap, cap), pl.ds(j * half, half)],
            sems.at[k],
        )

    for k in range(n):
        copy(k).start()
    step = 256 // cap
    for lo in range(0, sources, step):
        for k in range(3 * lo, 3 * (lo + step)):
            copy(k).wait()
        at = slice(lo * cap, (lo + step) * cap)
        gate = held[at, :half].astype(F32)
        up = held[at, half : 2 * half].astype(F32)
        down = held[at, 2 * half :].astype(F32)
        sig = jax.nn.sigmoid(gate)
        active = gate * sig
        hid = (active * up).astype(BF)
        ggp = (down * up * sig * (1.0 + gate * (1.0 - sig))).astype(BF)
        gup = (down * active).astype(BF)
        acts_ref[at, :half] = hid
        acts_ref[at, half : 2 * half] = ggp
        acts_ref[at, 2 * half :] = gup
        out = dot_nt(hid, wd_ref[...]).astype(BF)
        back = (dot_nt(ggp, wg_ref[...]) + dot_nt(gup, wu_ref[...])).astype(BF)
        ret_ref[lo : lo + step, :cap, :] = out.reshape(step, cap, dsl)
        ret_ref[lo : lo + step, cap:, :] = back.reshape(step, cap, dsl)


def grads_kernel(cap, own_ref, other_ref, acts_own, acts_other, gg_ref, gu_ref, gd_ref):
    sources, _, dsl = own_ref.shape
    half = gg_ref.shape[1]
    rows = sources * cap

    def both(first, lo):
        a = own_ref[:, first : first + cap, :].reshape(rows, dsl)
        b = other_ref[:, first : first + cap, :].reshape(rows, dsl)
        return dot_tn(a, acts_own[:, lo : lo + half]) + dot_tn(
            b, acts_other[:, lo : lo + half]
        )

    gg_ref[...] = both(0, half).astype(BF)
    gu_ref[...] = both(0, 2 * half).astype(BF)
    gd_ref[...] = both(cap, 0).astype(BF)


def combine_kernel(experts, cap, ret_ref, routes_ref, weight_ref, out_ref, grad_ref):
    dsl = out_ref.shape[0]
    picks = pickers(routes_ref[...], experts, cap)
    weight = weight_ref[...]
    out = ret_ref[:, :cap, :].reshape(experts * cap, dsl)
    back = ret_ref[:, cap:, :].reshape(experts * cap, dsl)
    out_ref[...] = sum(
        dot_tn(out, picks[k]) * weight[k : k + 1, :] for k in range(2)
    ).astype(BF)
    grad_ref[...] = dot_tn(back, picks[0] + picks[1]).astype(BF)


def per_device(tokens, routes, route_weight, w_gate, w_up, w_down, cotangent):
    ntok, dsl = tokens.shape
    top = routes.shape[1]
    n_expert = lax.axis_size("expert")
    experts = n_expert // 2
    half = w_gate.shape[1]
    cap = 2 * max(1, ntok * top // experts)
    rows = experts * cap
    shape = jax.ShapeDtypeStruct
    any_space = pl.BlockSpec(memory_space=pl.ANY)
    vmem = pl.BlockSpec(memory_space=pltpu.VMEM)
    cores = [list(range(c, n_expert, 2)) for c in range(2)]
    swap = [(i, i ^ 1) for i in range(n_expert)]
    flops = 2 * rows * dsl * half

    def exchange(a):
        return lax.all_to_all(
            a, "expert", 0, 0, axis_index_groups=cores, tiled=True
        )

    routes_t, weight_t, w_down_t = routes.T, route_weight.T, w_down.T
    block = shape((experts, 2 * cap, dsl), BF)
    send = pl.pallas_call(
        functools.partial(send_kernel, experts, cap),
        out_shape=block,
        compiler_params=params(),
        cost_estimate=cost(4 * rows * ntok * dsl, 2 * rows * dsl * 4),
    )(tokens.T, cotangent.T, routes_t, weight_t)
    own = exchange(send)
    other = lax.ppermute(own, "expert", swap)

    n = 3 * experts

    def terms(block_rows):
        return pl.pallas_call(
            functools.partial(terms_kernel, cap),
            out_shape=[shape((cap, half), BF)] * n,
            in_specs=[vmem] * 4,
            out_specs=[any_space] * n,
            scratch_shapes=[
                pltpu.VMEM((rows, 3 * half), BF),
                pltpu.SemaphoreType.DMA((n,)),
            ],
            compiler_params=params(),
            cost_estimate=cost(3 * flops, 2 * rows * (dsl * 2 + 3 * half)),
        )(block_rows, w_gate, w_up, w_down_t)

    sums = lax.psum(list(terms(own)) + list(terms(other)), "dp")

    def back(pieces):
        return pl.pallas_call(
            functools.partial(back_kernel, cap, n),
            out_shape=[shape((rows, 3 * half), BF), block],
            in_specs=[any_space] * n + [vmem] * 3,
            out_specs=[vmem] * 2,
            scratch_shapes=[
                pltpu.VMEM((rows, 3 * half), BF),
                pltpu.SemaphoreType.DMA((n,)),
            ],
            compiler_params=params(),
            cost_estimate=cost(3 * flops, 2 * rows * (dsl * 2 + 6 * half)),
        )(*pieces, w_gate, w_up, w_down_t)

    acts_other, ret_other = back(sums[n:])
    theirs = lax.ppermute(ret_other, "expert", swap)
    acts_own, ret_own = back(sums[:n])
    both = (ret_own.astype(F32) + theirs.astype(F32)).astype(BF)
    ret = exchange(both)
    grad_gate, grad_up, grad_down_t = pl.pallas_call(
        functools.partial(grads_kernel, cap),
        out_shape=[shape((dsl, half), BF)] * 3,
        compiler_params=params(),
        cost_estimate=cost(6 * flops, 4 * rows * (dsl * 2 + 3 * half)),
    )(own, other, acts_own, acts_other)
    output_t, grad_tokens_t = pl.pallas_call(
        functools.partial(combine_kernel, experts, cap),
        out_shape=[shape((dsl, ntok), BF)] * 2,
        compiler_params=params(),
        cost_estimate=cost(6 * rows * ntok * dsl, 2 * rows * dsl * 4),
    )(ret, routes_t, weight_t)
    return output_t.T, grad_tokens_t.T, grad_gate, grad_up, grad_down_t.T


def solution(mesh):
    return jax.shard_map(
        per_device,
        mesh=mesh,
        in_specs=(
            P("expert", "dp"),
            P("expert", None),
            P("expert", None),
            P("dp", "expert"),
            P("dp", "expert"),
            P("expert", "dp"),
            P("expert", "dp"),
        ),
        out_specs=(
            P("expert", "dp"),
            P("expert", "dp"),
            P("dp", "expert"),
            P("dp", "expert"),
            P("expert", "dp"),
        ),
        check_vma=False,
    )
```

```python
import functools

import jax
import jax.numpy as jnp
from jax import lax
from jax.experimental import pallas as pl
from jax.experimental.pallas import tpu as pltpu
from jax.sharding import PartitionSpec as P

BF = jnp.bfloat16
F32 = jnp.float32
VMEM_BYTES = 24 * 1024 * 1024


def dot_nn(a, b):
    return lax.dot_general(a, b, (((1,), (0,)), ((), ())), preferred_element_type=F32)


def dot_nt(a, b):
    return lax.dot_general(a, b, (((1,), (1,)), ((), ())), preferred_element_type=F32)


def dot_tn(a, b):
    return lax.dot_general(a, b, (((0,), (0,)), ((), ())), preferred_element_type=F32)


def params(**more):
    return pltpu.CompilerParams(vmem_limit_bytes=VMEM_BYTES, **more)


def cost(flops, moved):
    return pl.CostEstimate(flops=flops, bytes_accessed=moved, transcendentals=0)


def pickers(routes, experts, cap):
    top, ntok = routes.shape
    names = lax.broadcasted_iota(jnp.int32, (experts, ntok), 0)
    hits = [routes[k : k + 1, :] == names for k in range(top)]
    mask = sum(jnp.where(h, 1.0, 0.0) for h in hits)
    before = lax.broadcasted_iota(jnp.int32, (ntok, ntok), 0) < lax.broadcasted_iota(
        jnp.int32, (ntok, ntok), 1
    )
    slot = dot_nn(mask.astype(BF), jnp.where(before, 1.0, 0.0).astype(BF))
    want = lax.broadcasted_iota(jnp.int32, (experts, cap, ntok), 1).astype(F32)
    picks = []
    for h in hits:
        own = jnp.where(h, slot, -1.0)
        own = jnp.broadcast_to(own[:, None, :], (experts, cap, ntok))
        pick = jnp.where(own == want, 1.0, 0.0)
        picks.append(pick.reshape(experts * cap, ntok).astype(BF))
    return picks


def send_kernel(
    experts, cap, tok_hbm, cot_hbm, routes_hbm, weight_hbm, wg_hbm, wu_hbm, wd_hbm,
    out_ref, stack_hbm, tok_ref, cot_ref, routes_ref, weight_ref, sems,
):
    dsl, ntok = tok_ref.shape
    pairs = (
        (routes_hbm, routes_ref),
        (tok_hbm, tok_ref),
        (weight_hbm, weight_ref),
        (cot_hbm, cot_ref),
        (wg_hbm, stack_hbm.at[0]),
        (wu_hbm, stack_hbm.at[1]),
        (wd_hbm, stack_hbm.at[2]),
    )
    copies = [
        pltpu.make_async_copy(src, dst, sems.at[i])
        for i, (src, dst) in enumerate(pairs)
    ]
    for c in copies:
        c.start()
    copies[0].wait()
    picks = pickers(routes_ref[...], experts, cap)
    copies[1].wait()
    x = dot_nt(picks[0] + picks[1], tok_ref[...]).astype(BF)
    out_ref[:, :cap, :] = x.reshape(experts, cap, dsl)
    copies[2].wait()
    copies[3].wait()
    cot = cot_ref[...].astype(F32)
    weight = weight_ref[...]
    dy = sum(
        dot_nt(picks[k], (cot * weight[k : k + 1, :]).astype(BF)) for k in range(2)
    ).astype(BF)
    out_ref[:, cap:, :] = dy.reshape(experts, cap, dsl)
    for c in copies[4:]:
        c.wait()


def terms_kernel(cap, rows_ref, own_ref, other_ref, *rest):
    sources, _, dsl = rows_ref.shape
    outs, (held, sems) = rest[:-2], rest[-2:]
    half = own_ref.shape[2]
    step = 256 // cap
    copies = []
    for lo in range(0, sources, step):
        x = rows_ref[lo : lo + step, :cap, :].reshape(step * cap, dsl)
        dy = rows_ref[lo : lo + step, cap:, :].reshape(step * cap, dsl)
        at = slice(lo * cap, (lo + step) * cap)
        for q in range(6):
            j, h = divmod(q, 2)
            w = (own_ref, other_ref)[h][j]
            left = dy if j == 2 else x
            held[at, q * half : (q + 1) * half] = dot_nn(left, w).astype(BF)
            for i in range(lo, lo + step):
                k = 6 * i + q
                copies.append(
                    pltpu.make_async_copy(
                        held.at[pl.ds(i * cap, cap), pl.ds(q * half, half)],
                        outs[k],
                        sems.at[k],
                    )
                )
                copies[-1].start()
    for c in copies:
        c.wait()


def back_kernel(cap, n, *refs):
    pieces, (own_ref, other_ref, acts_ref, ret_ref, held, sems) = refs[:n], refs[n:]
    sources = n // 6
    dsl, half = own_ref.shape[1:]

    def copy(k):
        i, q = divmod(k, 6)
        return pltpu.make_async_copy(
            pieces[k],
            held.at[pl.ds(i * cap, cap), pl.ds(q * half, half)],
            sems.at[k],
        )

    for k in range(n):
        copy(k).start()
    step = 256 // cap
    for lo in range(0, sources, step):
        for k in range(6 * lo, 6 * (lo + step)):
            copy(k).wait()
        at = slice(lo * cap, (lo + step) * cap)
        out = back = None
        for h, w_ref in enumerate((own_ref, other_ref)):
            gate, up, down = (
                held[at, (2 * j + h) * half : (2 * j + h + 1) * half].astype(F32)
                for j in range(3)
            )
            sig = jax.nn.sigmoid(gate)
            active = gate * sig
            hid = (active * up).astype(BF)
            ggp = (down * up * sig * (1.0 + gate * (1.0 - sig))).astype(BF)
            gup = (down * active).astype(BF)
            for j, a in enumerate((ggp, gup, hid)):
                acts_ref[at, (3 * h + j) * half : (3 * h + j + 1) * half] = a
            part = dot_nt(hid, w_ref[2])
            out = part if out is None else out + part
            part = dot_nt(ggp, w_ref[0]) + dot_nt(gup, w_ref[1])
            back = part if back is None else back + part
        ret_ref[lo : lo + step, :cap, :] = out.astype(BF).reshape(step, cap, dsl)
        ret_ref[lo : lo + step, cap:, :] = back.astype(BF).reshape(step, cap, dsl)


def grad_of(cap, rows_ref, acts_ref, j):
    sources, _, dsl = rows_ref.shape
    half = acts_ref.shape[1] // 3
    first = cap if j == 2 else 0
    left = rows_ref[:, first : first + cap, :].reshape(sources * cap, dsl)
    return dot_tn(left, acts_ref[:, j * half : (j + 1) * half])


def other_grads_kernel(cap, rows_ref, acts_ref, out_ref):
    for j in range(3):
        out_ref[j] = grad_of(cap, rows_ref, acts_ref, j).astype(BF)


def own_grads_kernel(cap, rows_ref, acts_ref, theirs_ref, *outs):
    for j in range(3):
        part = grad_of(cap, rows_ref, acts_ref, j)
        outs[j][...] = (part + theirs_ref[j].astype(F32)).astype(BF)


def combine_kernel(experts, cap, ret_ref, routes_ref, weight_ref, out_ref, grad_ref):
    dsl = out_ref.shape[0]
    picks = pickers(routes_ref[...], experts, cap)
    weight = weight_ref[...]
    out = ret_ref[:, :cap, :].reshape(experts * cap, dsl)
    back = ret_ref[:, cap:, :].reshape(experts * cap, dsl)
    out_ref[...] = sum(
        dot_tn(out, picks[k]) * weight[k : k + 1, :] for k in range(2)
    ).astype(BF)
    grad_ref[...] = dot_tn(back, picks[0] + picks[1]).astype(BF)


def per_device(tokens, routes, route_weight, w_gate, w_up, w_down, cotangent):
    ntok, dsl = tokens.shape
    top = routes.shape[1]
    n_expert = lax.axis_size("expert")
    experts = n_expert // 2
    half = w_gate.shape[1]
    cap = 2 * max(1, ntok * top // experts)
    rows = experts * cap
    shape = jax.ShapeDtypeStruct
    hbm = pl.BlockSpec(memory_space=pltpu.HBM)
    vmem = pl.BlockSpec(memory_space=pltpu.VMEM)
    cores = [list(range(c, n_expert, 2)) for c in range(2)]
    swap = [(i, i ^ 1) for i in range(n_expert)]
    flops = 2 * rows * dsl * half

    def in_hbm(a):
        return pltpu.with_memory_space_constraint(a, pltpu.HBM)

    def exchange(a):
        return lax.all_to_all(a, "expert", 0, 0, axis_index_groups=cores, tiled=True)

    routes_t, weight_t = routes.T, route_weight.T
    block = shape((experts, 2 * cap, dsl), BF)
    stack = shape((3, dsl, half), BF)
    send, w_own = pl.pallas_call(
        functools.partial(send_kernel, experts, cap),
        out_shape=[block, stack],
        in_specs=[hbm] * 7,
        out_specs=[vmem, pl.BlockSpec(memory_space=pl.ANY)],
        scratch_shapes=[
            pltpu.VMEM((dsl, ntok), BF),
            pltpu.VMEM((dsl, ntok), BF),
            pltpu.VMEM((top, ntok), jnp.int32),
            pltpu.VMEM((top, ntok), F32),
            pltpu.SemaphoreType.DMA((7,)),
        ],
        compiler_params=params(),
        cost_estimate=cost(4 * rows * ntok * dsl, 2 * rows * dsl * 4),
    )(
        *(
            in_hbm(a)
            for a in (
                tokens.T, cotangent.T, routes_t, weight_t, w_gate, w_up, w_down.T
            )
        )
    )
    got = exchange(send)
    w_other = lax.ppermute(w_own, "expert", swap)

    n = 6 * experts
    pieces = pl.pallas_call(
        functools.partial(terms_kernel, cap),
        out_shape=[pltpu.HBM((cap, half), BF)] * n,
        in_specs=[vmem] * 3,
        out_specs=[hbm] * n,
        scratch_shapes=[
            pltpu.VMEM((rows, 6 * half), BF),
            pltpu.SemaphoreType.DMA((n,)),
        ],
        compiler_params=params(),
        cost_estimate=cost(6 * flops, 2 * rows * (dsl * 2 + 6 * half)),
    )(got, w_own, w_other)
    sums = [in_hbm(a) for a in lax.psum(list(pieces), "dp")]
    acts, ret = pl.pallas_call(
        functools.partial(back_kernel, cap, n),
        out_shape=[shape((rows, 6 * half), BF), block],
        in_specs=[hbm] * n + [vmem] * 2,
        out_specs=[vmem] * 2,
        scratch_shapes=[
            pltpu.VMEM((rows, 6 * half), BF),
            pltpu.SemaphoreType.DMA((n,)),
        ],
        compiler_params=params(),
        cost_estimate=cost(6 * flops, 2 * rows * (dsl * 2 + 12 * half)),
    )(*sums, w_own, w_other)
    ret = exchange(ret)

    whole = [
        pl.BlockSpec(block.shape, lambda i: (0, 0, 0)),
        pl.BlockSpec((rows, 3 * half), lambda i: (0, 1)),
    ]
    half_cost = cost(3 * flops, 2 * rows * (dsl * 2 + 3 * half))
    for_other = pl.pallas_call(
        functools.partial(other_grads_kernel, cap),
        grid=(1,),
        out_shape=stack,
        in_specs=whole,
        out_specs=pl.BlockSpec(stack.shape, lambda i: (0, 0, 0)),
        compiler_params=params(),
        cost_estimate=half_cost,
    )(got, acts)
    theirs = lax.ppermute(for_other, "expert", swap)
    whole[1] = pl.BlockSpec((rows, 3 * half), lambda i: (0, 0))
    grad_gate, grad_up, grad_down_t = pl.pallas_call(
        functools.partial(own_grads_kernel, cap),
        grid=(1,),
        out_shape=[shape((dsl, half), BF)] * 3,
        in_specs=whole + [pl.BlockSpec(stack.shape, lambda i: (0, 0, 0))],
        out_specs=[pl.BlockSpec((dsl, half), lambda i: (0, 0))] * 3,
        compiler_params=params(),
        cost_estimate=half_cost,
    )(got, acts, theirs)
    output_t, grad_tokens_t = pl.pallas_call(
        functools.partial(combine_kernel, experts, cap),
        out_shape=[shape((dsl, ntok), BF)] * 2,
        compiler_params=params(),
        cost_estimate=cost(6 * rows * ntok * dsl, 2 * rows * dsl * 4),
    )(ret, routes_t, weight_t)
    return output_t.T, grad_tokens_t.T, grad_gate, grad_up, grad_down_t.T


def solution(mesh):
    return jax.shard_map(
        per_device,
        mesh=mesh,
        in_specs=(
            P("expert", "dp"),
            P("expert", None),
            P("expert", None),
            P("dp", "expert"),
            P("dp", "expert"),
            P("expert", "dp"),
            P("expert", "dp"),
        ),
        out_specs=(
            P("expert", "dp"),
            P("expert", "dp"),
            P("dp", "expert"),
            P("dp", "expert"),
            P("expert", "dp"),
        ),
        check_vma=False,
    )
```

```python
import functools

import jax
import jax.numpy as jnp
from jax import lax
from jax.experimental import pallas as pl
from jax.experimental.pallas import tpu as pltpu
from jax.sharding import PartitionSpec as P

BF = jnp.bfloat16
F32 = jnp.float32
VMEM_BYTES = 24 * 1024 * 1024


def dot_nn(a, b):
    return lax.dot_general(a, b, (((1,), (0,)), ((), ())), preferred_element_type=F32)


def dot_nt(a, b):
    return lax.dot_general(a, b, (((1,), (1,)), ((), ())), preferred_element_type=F32)


def dot_tn(a, b):
    return lax.dot_general(a, b, (((0,), (0,)), ((), ())), preferred_element_type=F32)


def params(**more):
    return pltpu.CompilerParams(vmem_limit_bytes=VMEM_BYTES, **more)


def cost(flops, moved):
    return pl.CostEstimate(flops=flops, bytes_accessed=moved, transcendentals=0)


def pickers(routes, experts, cap):
    top, ntok = routes.shape
    names = lax.broadcasted_iota(jnp.int32, (experts, ntok), 0)
    hits = [routes[k : k + 1, :] == names for k in range(top)]
    mask = sum(jnp.where(h, 1.0, 0.0) for h in hits)
    before = lax.broadcasted_iota(jnp.int32, (ntok, ntok), 0) < lax.broadcasted_iota(
        jnp.int32, (ntok, ntok), 1
    )
    slot = dot_nn(mask.astype(BF), jnp.where(before, 1.0, 0.0).astype(BF))
    want = lax.broadcasted_iota(jnp.int32, (experts, cap, ntok), 1).astype(F32)
    picks = []
    for h in hits:
        own = jnp.where(h, slot, -1.0)
        own = jnp.broadcast_to(own[:, None, :], (experts, cap, ntok))
        pick = jnp.where(own == want, 1.0, 0.0)
        picks.append(pick.reshape(experts * cap, ntok).astype(BF))
    return picks


LANES = 128


def tiles(ref, lo, hi, cap, which):
    return jnp.concatenate(
        [
            ref[lo:hi, t * cap : (t + 1) * cap, :].reshape((hi - lo) * cap, LANES)
            for t in which
        ],
        axis=1,
    )


def put_tile(ref, lo, hi, cap, t, value):
    ref[lo:hi, t * cap : (t + 1) * cap, :] = value.reshape(hi - lo, cap, LANES)


def layout(dsl):
    full = dsl // LANES
    assert 2 * (dsl - full * LANES) == LANES
    first = [*range(full), 2 * full]
    return full * LANES, first, [*range(full, 2 * full), 2 * full]


def send_kernel(
    experts, cap, tok_hbm, cot_hbm, routes_hbm, weight_hbm, wg_hbm, wu_hbm, wd_hbm,
    out_ref, stack_hbm, tok_ref, cot_ref, routes_ref, weight_ref, zeros, sems,
):
    dsl, ntok = tok_ref.shape
    main, first, _ = layout(dsl)
    tail = dsl - main
    zeros[...] = jnp.zeros_like(zeros)
    pairs = (
        (routes_hbm, routes_ref),
        (tok_hbm, tok_ref),
        (weight_hbm, weight_ref),
        (cot_hbm, cot_ref),
        (wg_hbm, stack_hbm.at[0, pl.ds(0, dsl)]),
        (wu_hbm, stack_hbm.at[1, pl.ds(0, dsl)]),
        (wd_hbm.at[pl.ds(0, main)], stack_hbm.at[2, pl.ds(0, main)]),
        (wd_hbm.at[pl.ds(main, tail)], stack_hbm.at[2, pl.ds(dsl, tail)]),
        (zeros, stack_hbm.at[0, pl.ds(dsl, tail)]),
        (zeros, stack_hbm.at[1, pl.ds(dsl, tail)]),
        (zeros, stack_hbm.at[2, pl.ds(main, tail)]),
    )
    copies = [
        pltpu.make_async_copy(src, dst, sems.at[i])
        for i, (src, dst) in enumerate(pairs)
    ]
    for c in copies:
        c.start()
    copies[0].wait()
    picks = pickers(routes_ref[...], experts, cap)
    for c in copies[1:4]:
        c.wait()
    tok = tok_ref[...]
    cot = cot_ref[...].astype(F32)
    weight = weight_ref[...]
    rows = None
    for k, pick in enumerate(picks):
        dy = (cot * weight[k : k + 1, :]).astype(BF)
        right = jnp.concatenate([tok[:main], dy[:main], tok[main:], dy[main:]], axis=0)
        part = dot_nt(pick, right)
        rows = part if rows is None else rows + part
    rows = rows.astype(BF)
    for t in range(2 * len(first) - 1):
        put_tile(out_ref, 0, experts, cap, t, rows[:, t * LANES : (t + 1) * LANES])
    for c in copies[4:]:
        c.wait()


def terms_kernel(dsl, cap, rows_ref, own_ref, other_ref, *rest):
    sources = rows_ref.shape[0]
    outs, (held, sems) = rest[:-2], rest[-2:]
    _, first, second = layout(dsl)
    half = own_ref.shape[2]
    step = 256 // cap
    copies = []
    for lo in range(0, sources, step):
        x = tiles(rows_ref, lo, lo + step, cap, first)
        dy = tiles(rows_ref, lo, lo + step, cap, second)
        at = slice(lo * cap, (lo + step) * cap)
        for q in range(6):
            j, h = divmod(q, 2)
            w = (own_ref, other_ref)[h][j]
            left = dy if j == 2 else x
            held[at, q * half : (q + 1) * half] = dot_nn(left, w).astype(BF)
            for i in range(lo, lo + step):
                k = 6 * i + q
                copies.append(
                    pltpu.make_async_copy(
                        held.at[pl.ds(i * cap, cap), pl.ds(q * half, half)],
                        outs[k],
                        sems.at[k],
                    )
                )
                copies[-1].start()
    for c in copies:
        c.wait()


def back_kernel(dsl, cap, n, *refs):
    pieces, (own_hbm, other_hbm, acts_ref, ret_hbm, held, own_ref, other_ref, ret_ref, sems) = (
        refs[:n],
        refs[n:],
    )
    sources = n // 6
    half = own_ref.shape[2]
    main, first, _ = layout(dsl)
    full = main // LANES

    def copy(k):
        i, q = divmod(k, 6)
        return pltpu.make_async_copy(
            pieces[k],
            held.at[pl.ds(i * cap, cap), pl.ds(q * half, half)],
            sems.at[k],
        )

    weights = [
        pltpu.make_async_copy(own_hbm, own_ref, sems.at[n]),
        pltpu.make_async_copy(other_hbm, other_ref, sems.at[n + 1]),
    ]
    away = []
    step = 256 // cap
    for k in range(6 * step):
        copy(k).start()
    for c in weights:
        c.start()
    for k in range(6 * step, n):
        copy(k).start()
    for lo in range(0, sources, step):
        for k in range(6 * lo, 6 * (lo + step)):
            copy(k).wait()
        at = slice(lo * cap, (lo + step) * cap)
        out = back = None
        for h, w_ref in enumerate((own_ref, other_ref)):
            gate, up, down = (
                held[at, (2 * j + h) * half : (2 * j + h + 1) * half].astype(F32)
                for j in range(3)
            )
            sig = jax.nn.sigmoid(gate)
            active = gate * sig
            hid = (active * up).astype(BF)
            ggp = (down * up * sig * (1.0 + gate * (1.0 - sig))).astype(BF)
            gup = (down * active).astype(BF)
            for j, a in enumerate((ggp, gup, hid)):
                acts_ref[at, (3 * h + j) * half : (3 * h + j + 1) * half] = a
            if lo == 0:
                weights[h].wait()
            part = dot_nt(hid, w_ref[2])
            out = part if out is None else out + part
            part = dot_nt(ggp, w_ref[0]) + dot_nt(gup, w_ref[1])
            back = part if back is None else back + part
        hi = lo + step
        for t in range(full):
            lanes = slice(t * LANES, (t + 1) * LANES)
            put_tile(ret_ref, lo, hi, cap, t, back[:, lanes].astype(BF))
            put_tile(ret_ref, lo, hi, cap, full + t, out[:, lanes].astype(BF))
        last = back[:, main:] + out[:, main:]
        put_tile(ret_ref, lo, hi, cap, 2 * full, last.astype(BF))
        blocks = pl.ds(lo, step)
        away.append(
            pltpu.make_async_copy(
                ret_ref.at[blocks], ret_hbm.at[blocks], sems.at[n + 2 + len(away)]
            )
        )
        away[-1].start()
    for c in away:
        c.wait()


def grad_of(dsl, cap, rows_ref, acts_ref, j):
    sources = rows_ref.shape[0]
    half = acts_ref.shape[1] // 3
    main, first, second = layout(dsl)
    left = tiles(rows_ref, 0, sources, cap, second if j == 2 else first)
    grad = dot_tn(left, acts_ref[:, j * half : (j + 1) * half])
    if j == 2:
        return jnp.concatenate([grad[:main], grad[dsl:]], axis=0)
    return grad[:dsl]


def other_grads_kernel(dsl, cap, rows_ref, acts_ref, out_ref):
    for j in range(3):
        out_ref[j] = grad_of(dsl, cap, rows_ref, acts_ref, j).astype(BF)


def own_grads_kernel(dsl, cap, rows_ref, acts_ref, theirs_ref, *outs):
    for j in range(3):
        part = grad_of(dsl, cap, rows_ref, acts_ref, j)
        outs[j][...] = (part + theirs_ref[j].astype(F32)).astype(BF)


def combine_kernel(experts, cap, ret_ref, routes_ref, weight_ref, _, out_ref, grad_ref):
    dsl = out_ref.shape[0]
    main, first, _ = layout(dsl)
    tail = dsl - main
    picks = pickers(routes_ref[...], experts, cap)
    weight = weight_ref[...]
    rows = tiles(ret_ref, 0, experts, cap, range(2 * len(first) - 1))
    out = back = None
    for k, pick in enumerate(picks):
        got = dot_tn(rows, pick)
        b = jnp.concatenate([got[:main], got[2 * main : 2 * main + tail]], axis=0)
        o = jnp.concatenate([got[main : 2 * main], got[2 * main + tail :]], axis=0)
        o = o * weight[k : k + 1, :]
        out = o if out is None else out + o
        back = b if back is None else back + b
    out_ref[...] = out.astype(BF)
    grad_ref[...] = back.astype(BF)


def per_device(tokens, routes, route_weight, w_gate, w_up, w_down, cotangent):
    ntok, dsl = tokens.shape
    top = routes.shape[1]
    n_expert = lax.axis_size("expert")
    experts = n_expert // 2
    half = w_gate.shape[1]
    cap = 2 * max(1, ntok * top // experts)
    rows = experts * cap
    shape = jax.ShapeDtypeStruct
    hbm = pl.BlockSpec(memory_space=pltpu.HBM)
    vmem = pl.BlockSpec(memory_space=pltpu.VMEM)
    cores = [list(range(c, n_expert, 2)) for c in range(2)]
    swap = [(i, i ^ 1) for i in range(n_expert)]
    flops = 2 * rows * dsl * half

    def in_hbm(a):
        return pltpu.with_memory_space_constraint(a, pltpu.HBM)

    def exchange(a):
        return lax.all_to_all(a, "expert", 0, 0, axis_index_groups=cores, tiled=True)

    routes_t, weight_t = routes.T, route_weight.T
    main, first, _ = layout(dsl)
    block = shape((experts, (2 * len(first) - 1) * cap, LANES), BF)
    padded = (3, main + LANES, half)
    stack = shape((3, dsl, half), BF)
    send, w_own = pl.pallas_call(
        functools.partial(send_kernel, experts, cap),
        out_shape=[block, pltpu.HBM(padded, BF)],
        in_specs=[hbm] * 7,
        out_specs=[vmem, hbm],
        scratch_shapes=[
            pltpu.VMEM((dsl, ntok), BF),
            pltpu.VMEM((dsl, ntok), BF),
            pltpu.VMEM((top, ntok), jnp.int32),
            pltpu.VMEM((top, ntok), F32),
            pltpu.VMEM((dsl - main, half), BF),
            pltpu.SemaphoreType.DMA((11,)),
        ],
        compiler_params=params(),
        cost_estimate=cost(4 * rows * ntok * dsl, 2 * rows * dsl * 4),
    )(
        *(
            in_hbm(a)
            for a in (
                tokens.T, cotangent.T, routes_t, weight_t, w_gate, w_up, w_down.T
            )
        )
    )
    got = exchange(send)
    w_other = lax.ppermute(w_own, "expert", swap)

    n = 6 * experts
    pieces = pl.pallas_call(
        functools.partial(terms_kernel, dsl, cap),
        out_shape=[pltpu.HBM((cap, half), BF)] * n,
        in_specs=[vmem] * 3,
        out_specs=[hbm] * n,
        scratch_shapes=[
            pltpu.VMEM((rows, 6 * half), BF),
            pltpu.SemaphoreType.DMA((n,)),
        ],
        compiler_params=params(),
        cost_estimate=cost(6 * flops, 2 * rows * (dsl * 2 + 6 * half)),
    )(got, w_own, w_other)
    sums = [in_hbm(a) for a in lax.psum(list(pieces), "dp")]
    acts, ret = pl.pallas_call(
        functools.partial(back_kernel, dsl, cap, n),
        out_shape=[shape((rows, 6 * half), BF), pltpu.HBM(block.shape, BF)],
        in_specs=[hbm] * (n + 2),
        out_specs=[vmem, hbm],
        scratch_shapes=[
            pltpu.VMEM((rows, 6 * half), BF),
            pltpu.VMEM(padded, BF),
            pltpu.VMEM(padded, BF),
            pltpu.VMEM(block.shape, BF),
            pltpu.SemaphoreType.DMA((n + 2 + rows // 256,)),
        ],
        compiler_params=params(),
        cost_estimate=cost(6 * flops, 2 * rows * (dsl * 2 + 12 * half)),
    )(*sums, in_hbm(w_own), in_hbm(w_other))
    ret = exchange(ret)

    whole = [
        pl.BlockSpec(block.shape, lambda i: (0, 0, 0)),
        pl.BlockSpec((rows, 3 * half), lambda i: (0, 1)),
    ]
    half_cost = cost(3 * flops, 2 * rows * (dsl * 2 + 3 * half))
    for_other = pl.pallas_call(
        functools.partial(other_grads_kernel, dsl, cap),
        grid=(1,),
        out_shape=stack,
        in_specs=whole,
        out_specs=pl.BlockSpec(stack.shape, lambda i: (0, 0, 0)),
        compiler_params=params(),
        cost_estimate=half_cost,
    )(got, acts)
    theirs = lax.ppermute(for_other, "expert", swap)
    whole[1] = pl.BlockSpec((rows, 3 * half), lambda i: (0, 0))
    grad_gate, grad_up, grad_down_t = pl.pallas_call(
        functools.partial(own_grads_kernel, dsl, cap),
        grid=(1,),
        out_shape=[shape((dsl, half), BF)] * 3,
        in_specs=whole + [pl.BlockSpec(stack.shape, lambda i: (0, 0, 0))],
        out_specs=[pl.BlockSpec((dsl, half), lambda i: (0, 0))] * 3,
        compiler_params=params(),
        cost_estimate=half_cost,
    )(got, acts, theirs)
    output_t, grad_tokens_t = pl.pallas_call(
        functools.partial(combine_kernel, experts, cap),
        out_shape=[shape((dsl, ntok), BF)] * 2,
        in_specs=[vmem] * 3 + [hbm],
        out_specs=[vmem] * 2,
        compiler_params=params(),
        cost_estimate=cost(6 * rows * ntok * dsl, 2 * rows * dsl * 4),
    )(ret, routes_t, weight_t, in_hbm(grad_gate))
    return output_t.T, grad_tokens_t.T, grad_gate, grad_up, grad_down_t.T


def solution(mesh):
    return jax.shard_map(
        per_device,
        mesh=mesh,
        in_specs=(
            P("expert", "dp"),
            P("expert", None),
            P("expert", None),
            P("dp", "expert"),
            P("dp", "expert"),
            P("expert", "dp"),
            P("expert", "dp"),
        ),
        out_specs=(
            P("expert", "dp"),
            P("expert", "dp"),
            P("dp", "expert"),
            P("dp", "expert"),
            P("expert", "dp"),
        ),
        check_vma=False,
    )
```

```python
import functools

import jax
import jax.numpy as jnp
from jax import lax
from jax.experimental import pallas as pl
from jax.experimental.pallas import tpu as pltpu
from jax.sharding import PartitionSpec as P

BF = jnp.bfloat16
F32 = jnp.float32
VMEM_BYTES = 24 * 1024 * 1024


def dot_nn(a, b):
    return lax.dot_general(a, b, (((1,), (0,)), ((), ())), preferred_element_type=F32)


def dot_nt(a, b):
    return lax.dot_general(a, b, (((1,), (1,)), ((), ())), preferred_element_type=F32)


def dot_tn(a, b):
    return lax.dot_general(a, b, (((0,), (0,)), ((), ())), preferred_element_type=F32)


def params(**more):
    return pltpu.CompilerParams(vmem_limit_bytes=VMEM_BYTES, **more)


def cost(flops, moved):
    return pl.CostEstimate(flops=flops, bytes_accessed=moved, transcendentals=0)


def pickers(routes, experts, cap):
    top, ntok = routes.shape
    names = lax.broadcasted_iota(jnp.int32, (experts, ntok), 0)
    hits = [routes[k : k + 1, :] == names for k in range(top)]
    mask = sum(jnp.where(h, 1.0, 0.0) for h in hits)
    before = lax.broadcasted_iota(jnp.int32, (ntok, ntok), 0) < lax.broadcasted_iota(
        jnp.int32, (ntok, ntok), 1
    )
    slot = dot_nn(mask.astype(BF), jnp.where(before, 1.0, 0.0).astype(BF))
    want = lax.broadcasted_iota(jnp.int32, (experts, cap, ntok), 1).astype(F32)
    picks = []
    for h in hits:
        own = jnp.where(h, slot, -1.0)
        own = jnp.broadcast_to(own[:, None, :], (experts, cap, ntok))
        pick = jnp.where(own == want, 1.0, 0.0)
        picks.append(pick.reshape(experts * cap, ntok).astype(BF))
    return picks


def send_kernel(
    experts, cap, tok_hbm, cot_hbm, routes_hbm, weight_hbm, wg_hbm, wu_hbm, wd_hbm,
    out_ref, stack_hbm, tok_ref, cot_ref, routes_ref, weight_ref, sems,
):
    dsl, ntok = tok_ref.shape
    pairs = (
        (routes_hbm, routes_ref),
        (tok_hbm, tok_ref),
        (weight_hbm, weight_ref),
        (cot_hbm, cot_ref),
        (wg_hbm, stack_hbm.at[0]),
        (wu_hbm, stack_hbm.at[1]),
        (wd_hbm, stack_hbm.at[2]),
    )
    copies = [
        pltpu.make_async_copy(src, dst, sems.at[i])
        for i, (src, dst) in enumerate(pairs)
    ]
    for c in copies:
        c.start()
    copies[0].wait()
    picks = pickers(routes_ref[...], experts, cap)
    copies[1].wait()
    x = dot_nt(picks[0] + picks[1], tok_ref[...]).astype(BF)
    out_ref[:, :cap, :] = x.reshape(experts, cap, dsl)
    copies[2].wait()
    copies[3].wait()
    cot = cot_ref[...].astype(F32)
    weight = weight_ref[...]
    dy = sum(
        dot_nt(picks[k], (cot * weight[k : k + 1, :]).astype(BF)) for k in range(2)
    ).astype(BF)
    out_ref[:, cap:, :] = dy.reshape(experts, cap, dsl)
    for c in copies[4:]:
        c.wait()


def terms_kernel(cap, rows_ref, own_ref, other_ref, *rest):
    sources, _, dsl = rows_ref.shape
    outs, (held, sems) = rest[:-2], rest[-2:]
    half = own_ref.shape[2]
    step = 256 // cap
    copies = []
    for lo in range(0, sources, step):
        x = rows_ref[lo : lo + step, :cap, :].reshape(step * cap, dsl)
        dy = rows_ref[lo : lo + step, cap:, :].reshape(step * cap, dsl)
        at = slice(lo * cap, (lo + step) * cap)
        for q in range(6):
            j, h = divmod(q, 2)
            w = (own_ref, other_ref)[h][j]
            left = dy if j == 2 else x
            held[at, q * half : (q + 1) * half] = dot_nn(left, w).astype(BF)
            for i in range(lo, lo + step):
                k = 6 * i + q
                copies.append(
                    pltpu.make_async_copy(
                        held.at[pl.ds(i * cap, cap), pl.ds(q * half, half)],
                        outs[k],
                        sems.at[k],
                    )
                )
                copies[-1].start()
    for c in copies:
        c.wait()


def back_kernel(cap, n, *refs):
    pieces = refs[:n]
    own_hbm, other_ref, acts_ref, ret_ref, held, own_ref, sems = refs[n:]
    sources = n // 6
    dsl, half = own_ref.shape[1:]
    weights = [
        pltpu.make_async_copy(own_hbm.at[j], own_ref.at[j], sems.at[n + j])
        for j in range(3)
    ]

    def copy(k):
        i, q = divmod(k, 6)
        return pltpu.make_async_copy(
            pieces[k],
            held.at[pl.ds(i * cap, cap), pl.ds(q * half, half)],
            sems.at[k],
        )

    step = 256 // cap
    for k in range(6 * step):
        copy(k).start()
    for c in weights:
        c.start()
    for k in range(6 * step, n):
        copy(k).start()
    for lo in range(0, sources, step):
        for k in range(6 * lo, 6 * (lo + step)):
            copy(k).wait()
        at = slice(lo * cap, (lo + step) * cap)
        out = back = None
        for h, w_ref in ((1, other_ref), (0, own_ref)):
            gate, up, down = (
                held[at, (2 * j + h) * half : (2 * j + h + 1) * half].astype(F32)
                for j in range(3)
            )
            sig = jax.nn.sigmoid(gate)
            active = gate * sig
            hid = (active * up).astype(BF)
            ggp = (down * up * sig * (1.0 + gate * (1.0 - sig))).astype(BF)
            gup = (down * active).astype(BF)
            for j, a in enumerate((ggp, gup, hid)):
                acts_ref[at, (3 * h + j) * half : (3 * h + j + 1) * half] = a
            if lo == 0 and h == 0:
                for c in weights:
                    c.wait()
            part = dot_nt(hid, w_ref[2])
            out = part if out is None else out + part
            part = dot_nt(ggp, w_ref[0]) + dot_nt(gup, w_ref[1])
            back = part if back is None else back + part
        ret_ref[lo : lo + step, :cap, :] = out.astype(BF).reshape(step, cap, dsl)
        ret_ref[lo : lo + step, cap:, :] = back.astype(BF).reshape(step, cap, dsl)


def grad_of(cap, rows_ref, acts_ref, j):
    sources, _, dsl = rows_ref.shape
    half = acts_ref.shape[1] // 3
    first = cap if j == 2 else 0
    left = rows_ref[:, first : first + cap, :].reshape(sources * cap, dsl)
    return dot_tn(left, acts_ref[:, j * half : (j + 1) * half])


def grads_kernel(cap, rows_ref, acts_ref, *rest):
    out_ref = rest[-1]
    for j in range(3):
        out_ref[j] = grad_of(cap, rows_ref, acts_ref, j).astype(out_ref.dtype)


def add_kernel(own_ref, theirs_ref, *outs):
    for j, out_ref in enumerate(outs):
        out_ref[...] = (own_ref[j] + theirs_ref[j].astype(F32)).astype(BF)


def combine_kernel(experts, cap, ret_ref, routes_ref, weight_ref, out_ref, grad_ref):
    dsl = out_ref.shape[0]
    picks = pickers(routes_ref[...], experts, cap)
    weight = weight_ref[...]
    out = ret_ref[:, :cap, :].reshape(experts * cap, dsl)
    back = ret_ref[:, cap:, :].reshape(experts * cap, dsl)
    out_ref[...] = sum(
        dot_tn(out, picks[k]) * weight[k : k + 1, :] for k in range(2)
    ).astype(BF)
    grad_ref[...] = dot_tn(back, picks[0] + picks[1]).astype(BF)


def per_device(tokens, routes, route_weight, w_gate, w_up, w_down, cotangent):
    ntok, dsl = tokens.shape
    top = routes.shape[1]
    n_expert = lax.axis_size("expert")
    experts = n_expert // 2
    half = w_gate.shape[1]
    cap = 2 * max(1, ntok * top // experts)
    rows = experts * cap
    shape = jax.ShapeDtypeStruct
    hbm = pl.BlockSpec(memory_space=pltpu.HBM)
    vmem = pl.BlockSpec(memory_space=pltpu.VMEM)
    cores = [list(range(c, n_expert, 2)) for c in range(2)]
    swap = [(i, i ^ 1) for i in range(n_expert)]
    flops = 2 * rows * dsl * half

    def in_hbm(a):
        return pltpu.with_memory_space_constraint(a, pltpu.HBM)

    def exchange(a):
        return lax.all_to_all(a, "expert", 0, 0, axis_index_groups=cores, tiled=True)

    routes_t, weight_t = routes.T, route_weight.T
    block = shape((experts, 2 * cap, dsl), BF)
    stack = shape((3, dsl, half), BF)
    send, w_own = pl.pallas_call(
        functools.partial(send_kernel, experts, cap),
        out_shape=[block, stack],
        in_specs=[hbm] * 7,
        out_specs=[vmem, pl.BlockSpec(memory_space=pl.ANY)],
        scratch_shapes=[
            pltpu.VMEM((dsl, ntok), BF),
            pltpu.VMEM((dsl, ntok), BF),
            pltpu.VMEM((top, ntok), jnp.int32),
            pltpu.VMEM((top, ntok), F32),
            pltpu.SemaphoreType.DMA((7,)),
        ],
        compiler_params=params(),
        cost_estimate=cost(4 * rows * ntok * dsl, 2 * rows * dsl * 4),
    )(
        *(
            in_hbm(a)
            for a in (
                tokens.T, cotangent.T, routes_t, weight_t, w_gate, w_up, w_down.T
            )
        )
    )
    got = exchange(send)
    w_other = lax.ppermute(w_own, "expert", swap)

    n = 6 * experts
    pieces = pl.pallas_call(
        functools.partial(terms_kernel, cap),
        out_shape=[pltpu.HBM((cap, half), BF)] * n,
        in_specs=[vmem] * 3,
        out_specs=[hbm] * n,
        scratch_shapes=[
            pltpu.VMEM((rows, 6 * half), BF),
            pltpu.SemaphoreType.DMA((n,)),
        ],
        compiler_params=params(),
        cost_estimate=cost(6 * flops, 2 * rows * (dsl * 2 + 6 * half)),
    )(got, w_own, w_other)
    sums = [in_hbm(a) for a in lax.psum(list(pieces), "dp")]
    acts, ret = pl.pallas_call(
        functools.partial(back_kernel, cap, n),
        out_shape=[shape((rows, 6 * half), BF), block],
        in_specs=[hbm] * (n + 1) + [vmem],
        out_specs=[vmem] * 2,
        scratch_shapes=[
            pltpu.VMEM((rows, 6 * half), BF),
            pltpu.VMEM(stack.shape, BF),
            pltpu.SemaphoreType.DMA((n + 3,)),
        ],
        compiler_params=params(),
        cost_estimate=cost(6 * flops, 2 * rows * (dsl * 2 + 12 * half)),
    )(*sums, in_hbm(w_own), w_other)
    ret = exchange(ret)

    def grads(part, dtype, *after):
        return pl.pallas_call(
            functools.partial(grads_kernel, cap),
            grid=(1,),
            out_shape=shape(stack.shape, dtype),
            in_specs=[
                pl.BlockSpec(block.shape, lambda i: (0, 0, 0)),
                pl.BlockSpec((rows, 3 * half), lambda i: (0, part)),
            ]
            + [hbm] * len(after),
            out_specs=pl.BlockSpec(stack.shape, lambda i: (0, 0, 0)),
            compiler_params=params(),
            cost_estimate=cost(3 * flops, 2 * rows * (dsl * 2 + 3 * half)),
        )(got, acts, *after)

    theirs = lax.ppermute(grads(1, BF, in_hbm(ret)), "expert", swap)
    own = grads(0, F32)
    output_t, grad_tokens_t = pl.pallas_call(
        functools.partial(combine_kernel, experts, cap),
        out_shape=[shape((dsl, ntok), BF)] * 2,
        compiler_params=params(),
        cost_estimate=cost(6 * rows * ntok * dsl, 2 * rows * dsl * 4),
    )(ret, routes_t, weight_t)
    grad_gate, grad_up, grad_down_t = pl.pallas_call(
        add_kernel,
        out_shape=[shape((dsl, half), BF)] * 3,
        compiler_params=params(),
        cost_estimate=cost(3 * dsl * half, 24 * dsl * half),
    )(own, theirs)
    return output_t.T, grad_tokens_t.T, grad_gate, grad_up, grad_down_t.T


def solution(mesh):
    return jax.shard_map(
        per_device,
        mesh=mesh,
        in_specs=(
            P("expert", "dp"),
            P("expert", None),
            P("expert", None),
            P("dp", "expert"),
            P("dp", "expert"),
            P("expert", "dp"),
            P("expert", "dp"),
        ),
        out_specs=(
            P("expert", "dp"),
            P("expert", "dp"),
            P("dp", "expert"),
            P("dp", "expert"),
            P("expert", "dp"),
        ),
        check_vma=False,
    )
```

```python
import functools

import jax
import jax.numpy as jnp
from jax import lax
from jax.experimental import pallas as pl
from jax.experimental.pallas import tpu as pltpu
from jax.sharding import PartitionSpec as P

BF = jnp.bfloat16
F32 = jnp.float32
VMEM_BYTES = 24 * 1024 * 1024


def dot_nn(a, b):
    return lax.dot_general(a, b, (((1,), (0,)), ((), ())), preferred_element_type=F32)


def dot_nt(a, b):
    return lax.dot_general(a, b, (((1,), (1,)), ((), ())), preferred_element_type=F32)


def dot_tn(a, b):
    return lax.dot_general(a, b, (((0,), (0,)), ((), ())), preferred_element_type=F32)


def params(**more):
    return pltpu.CompilerParams(vmem_limit_bytes=VMEM_BYTES, **more)


def cost(flops, moved):
    return pl.CostEstimate(flops=flops, bytes_accessed=moved, transcendentals=0)


def pickers(routes, experts, cap):
    top, ntok = routes.shape
    names = lax.broadcasted_iota(jnp.int32, (experts, ntok), 0)
    hits = [routes[k : k + 1, :] == names for k in range(top)]
    mask = sum(jnp.where(h, 1.0, 0.0) for h in hits)
    before = lax.broadcasted_iota(jnp.int32, (ntok, ntok), 0) < lax.broadcasted_iota(
        jnp.int32, (ntok, ntok), 1
    )
    slot = dot_nn(mask.astype(BF), jnp.where(before, 1.0, 0.0).astype(BF))
    want = lax.broadcasted_iota(jnp.int32, (experts, cap, ntok), 1).astype(F32)
    picks = []
    for h in hits:
        own = jnp.where(h, slot, -1.0)
        own = jnp.broadcast_to(own[:, None, :], (experts, cap, ntok))
        pick = jnp.where(own == want, 1.0, 0.0)
        picks.append(pick.reshape(experts * cap, ntok).astype(BF))
    return picks


LANES = 128


def tiles(ref, lo, hi, cap, which):
    return jnp.concatenate(
        [
            ref[lo:hi, t * cap : (t + 1) * cap, :].reshape((hi - lo) * cap, LANES)
            for t in which
        ],
        axis=1,
    )


def put_tile(ref, lo, hi, cap, t, value):
    ref[lo:hi, t * cap : (t + 1) * cap, :] = value.reshape(hi - lo, cap, LANES)


def layout(dsl):
    full = dsl // LANES
    assert 2 * (dsl - full * LANES) == LANES
    first = [*range(full), 2 * full]
    return full * LANES, first, [*range(full, 2 * full), 2 * full]


def send_kernel(
    experts, cap, tok_hbm, cot_hbm, routes_hbm, weight_hbm, wg_hbm, wu_hbm, wd_hbm,
    out_ref, stack_hbm, tok_ref, cot_ref, routes_ref, weight_ref, zeros, sems,
):
    dsl, ntok = tok_ref.shape
    main, first, _ = layout(dsl)
    tail = dsl - main
    zeros[...] = jnp.zeros_like(zeros)
    pairs = (
        (routes_hbm, routes_ref),
        (tok_hbm, tok_ref),
        (weight_hbm, weight_ref),
        (cot_hbm, cot_ref),
        (wg_hbm, stack_hbm.at[0, pl.ds(0, dsl)]),
        (wu_hbm, stack_hbm.at[1, pl.ds(0, dsl)]),
        (wd_hbm.at[pl.ds(0, main)], stack_hbm.at[2, pl.ds(0, main)]),
        (wd_hbm.at[pl.ds(main, tail)], stack_hbm.at[2, pl.ds(dsl, tail)]),
        (zeros, stack_hbm.at[0, pl.ds(dsl, tail)]),
        (zeros, stack_hbm.at[1, pl.ds(dsl, tail)]),
        (zeros, stack_hbm.at[2, pl.ds(main, tail)]),
    )
    copies = [
        pltpu.make_async_copy(src, dst, sems.at[i])
        for i, (src, dst) in enumerate(pairs)
    ]
    for c in copies:
        c.start()
    copies[0].wait()
    picks = pickers(routes_ref[...], experts, cap)
    for c in copies[1:4]:
        c.wait()
    tok = tok_ref[...]
    cot = cot_ref[...].astype(F32)
    weight = weight_ref[...]
    rows = None
    for k, pick in enumerate(picks):
        dy = (cot * weight[k : k + 1, :]).astype(BF)
        right = jnp.concatenate([tok[:main], dy[:main], tok[main:], dy[main:]], axis=0)
        part = dot_nt(pick, right)
        rows = part if rows is None else rows + part
    rows = rows.astype(BF)
    for t in range(2 * len(first) - 1):
        put_tile(out_ref, 0, experts, cap, t, rows[:, t * LANES : (t + 1) * LANES])
    for c in copies[4:]:
        c.wait()


def terms_kernel(dsl, cap, rows_ref, own_ref, other_ref, *rest):
    sources = rows_ref.shape[0]
    outs, (held, sems) = rest[:-2], rest[-2:]
    _, first, second = layout(dsl)
    half = own_ref.shape[2]
    step = 256 // cap
    copies = []
    for lo in range(0, sources, step):
        x = tiles(rows_ref, lo, lo + step, cap, first)
        dy = tiles(rows_ref, lo, lo + step, cap, second)
        at = slice(lo * cap, (lo + step) * cap)
        for q in range(6):
            j, h = divmod(q, 2)
            w = (own_ref, other_ref)[h][j]
            left = dy if j == 2 else x
            held[at, q * half : (q + 1) * half] = dot_nn(left, w).astype(BF)
            for i in range(lo, lo + step):
                k = 6 * i + q
                copies.append(
                    pltpu.make_async_copy(
                        held.at[pl.ds(i * cap, cap), pl.ds(q * half, half)],
                        outs[k],
                        sems.at[k],
                    )
                )
                copies[-1].start()
    for c in copies:
        c.wait()


def back_kernel(dsl, cap, n, *refs):
    pieces = refs[:n]
    own_ref, other_hbm, acts_ref, ret_ref, held, other_ref, sems = refs[n:]
    sources = n // 6
    weights = [
        pltpu.make_async_copy(other_hbm.at[j], other_ref.at[j], sems.at[n + j])
        for j in range(3)
    ]
    half = own_ref.shape[2]
    main, _, _ = layout(dsl)
    full = main // LANES
    step = 256 // cap

    def copies(lo, h):
        for i in range(lo, lo + step):
            for q in range(h, 6, 2):
                k = 6 * i + q
                yield pltpu.make_async_copy(pieces[k], held.at[q, i], sems.at[k])

    order = [(lo, h) for lo in range(0, sources, step) for h in range(2)]
    for lo, h in order:
        for c in copies(lo, h):
            c.start()
        if lo == 0 and h == 1:
            for c in weights:
                c.start()
    for lo, h in order:
        for c in copies(lo, h):
            c.wait()
        hi = lo + step
        at = slice(lo * cap, hi * cap)
        gate, up, down = (
            held[2 * j + h, lo:hi].reshape(step * cap, half).astype(F32)
            for j in range(3)
        )
        sig = jax.nn.sigmoid(gate)
        active = gate * sig
        hid = (active * up).astype(BF)
        ggp = (down * up * sig * (1.0 + gate * (1.0 - sig))).astype(BF)
        gup = (down * active).astype(BF)
        for j, a in enumerate((ggp, gup, hid)):
            acts_ref[at, (3 * h + j) * half : (3 * h + j + 1) * half] = a
        if lo == 0 and h == 1:
            for c in weights:
                c.wait()
        w_ref = (own_ref, other_ref)[h]
        part_out = dot_nt(hid, w_ref[2])
        part_back = dot_nt(ggp, w_ref[0]) + dot_nt(gup, w_ref[1])
        if h == 0:
            out, back = part_out, part_back
            continue
        out, back = out + part_out, back + part_back
        for t in range(full):
            lanes = slice(t * LANES, (t + 1) * LANES)
            put_tile(ret_ref, lo, hi, cap, t, back[:, lanes].astype(BF))
            put_tile(ret_ref, lo, hi, cap, full + t, out[:, lanes].astype(BF))
        last = back[:, main:] + out[:, main:]
        put_tile(ret_ref, lo, hi, cap, 2 * full, last.astype(BF))


def grad_of(dsl, cap, rows_ref, acts_ref, j):
    sources = rows_ref.shape[0]
    half = acts_ref.shape[1] // 3
    main, first, second = layout(dsl)
    left = tiles(rows_ref, 0, sources, cap, second if j == 2 else first)
    grad = dot_tn(left, acts_ref[:, j * half : (j + 1) * half])
    if j == 2:
        return jnp.concatenate([grad[:main], grad[dsl:]], axis=0)
    return grad[:dsl]


def grads_kernel(dsl, cap, rows_ref, acts_ref, *rest):
    out_ref = rest[-1]
    for j in range(3):
        out_ref[j] = grad_of(dsl, cap, rows_ref, acts_ref, j).astype(out_ref.dtype)


def add_kernel(own_ref, theirs_ref, *outs):
    for j, out_ref in enumerate(outs):
        out_ref[...] = (own_ref[j] + theirs_ref[j].astype(F32)).astype(BF)


def combine_kernel(experts, cap, ret_ref, routes_ref, weight_ref, out_ref, grad_ref):
    dsl = out_ref.shape[0]
    main, first, _ = layout(dsl)
    tail = dsl - main
    picks = pickers(routes_ref[...], experts, cap)
    weight = weight_ref[...]
    rows = tiles(ret_ref, 0, experts, cap, range(2 * len(first) - 1))
    out = back = None
    for k, pick in enumerate(picks):
        got = dot_tn(rows, pick)
        b = jnp.concatenate([got[:main], got[2 * main : 2 * main + tail]], axis=0)
        o = jnp.concatenate([got[main : 2 * main], got[2 * main + tail :]], axis=0)
        o = o * weight[k : k + 1, :]
        out = o if out is None else out + o
        back = b if back is None else back + b
    out_ref[...] = out.astype(BF)
    grad_ref[...] = back.astype(BF)


def per_device(tokens, routes, route_weight, w_gate, w_up, w_down, cotangent):
    ntok, dsl = tokens.shape
    top = routes.shape[1]
    n_expert = lax.axis_size("expert")
    experts = n_expert // 2
    half = w_gate.shape[1]
    cap = 2 * max(1, ntok * top // experts)
    rows = experts * cap
    shape = jax.ShapeDtypeStruct
    hbm = pl.BlockSpec(memory_space=pltpu.HBM)
    vmem = pl.BlockSpec(memory_space=pltpu.VMEM)
    cores = [list(range(c, n_expert, 2)) for c in range(2)]
    swap = [(i, i ^ 1) for i in range(n_expert)]
    flops = 2 * rows * dsl * half

    def in_hbm(a):
        return pltpu.with_memory_space_constraint(a, pltpu.HBM)

    def exchange(a):
        return lax.all_to_all(a, "expert", 0, 0, axis_index_groups=cores, tiled=True)

    routes_t, weight_t = routes.T, route_weight.T
    main, first, _ = layout(dsl)
    block = shape((experts, (2 * len(first) - 1) * cap, LANES), BF)
    padded = shape((3, main + LANES, half), BF)
    stack = shape((3, dsl, half), BF)
    send, w_own = pl.pallas_call(
        functools.partial(send_kernel, experts, cap),
        out_shape=[block, padded],
        in_specs=[hbm] * 7,
        out_specs=[vmem, pl.BlockSpec(memory_space=pl.ANY)],
        scratch_shapes=[
            pltpu.VMEM((dsl, ntok), BF),
            pltpu.VMEM((dsl, ntok), BF),
            pltpu.VMEM((top, ntok), jnp.int32),
            pltpu.VMEM((top, ntok), F32),
            pltpu.VMEM((dsl - main, half), BF),
            pltpu.SemaphoreType.DMA((11,)),
        ],
        compiler_params=params(),
        cost_estimate=cost(4 * rows * ntok * dsl, 2 * rows * dsl * 4),
    )(
        *(
            in_hbm(a)
            for a in (
                tokens.T, cotangent.T, routes_t, weight_t, w_gate, w_up, w_down.T
            )
        )
    )
    got = exchange(send)
    w_other = lax.ppermute(w_own, "expert", swap)

    n = 6 * experts
    pieces = pl.pallas_call(
        functools.partial(terms_kernel, dsl, cap),
        out_shape=[pltpu.HBM((cap, half), BF)] * n,
        in_specs=[vmem] * 3,
        out_specs=[hbm] * n,
        scratch_shapes=[
            pltpu.VMEM((rows, 6 * half), BF),
            pltpu.SemaphoreType.DMA((n,)),
        ],
        compiler_params=params(),
        cost_estimate=cost(6 * flops, 2 * rows * (dsl * 2 + 6 * half)),
    )(got, w_own, w_other)
    sums = [in_hbm(a) for a in lax.psum(list(pieces), "dp")]
    acts, ret = pl.pallas_call(
        functools.partial(back_kernel, dsl, cap, n),
        out_shape=[shape((rows, 6 * half), BF), block],
        in_specs=[hbm] * n + [vmem, hbm],
        out_specs=[vmem] * 2,
        scratch_shapes=[
            pltpu.VMEM((6, experts, cap, half), BF),
            pltpu.VMEM(padded.shape, BF),
            pltpu.SemaphoreType.DMA((n + 3,)),
        ],
        compiler_params=params(),
        cost_estimate=cost(6 * flops, 2 * rows * (dsl * 2 + 12 * half)),
    )(*sums, w_own, in_hbm(w_other))
    ret = exchange(ret)

    parked = in_hbm(got)

    def grads(part, dtype, *after):
        return pl.pallas_call(
            functools.partial(grads_kernel, dsl, cap),
            grid=(1,),
            out_shape=shape(stack.shape, dtype),
            in_specs=[
                pl.BlockSpec(block.shape, lambda i: (0, 0, 0)),
                pl.BlockSpec((rows, 3 * half), lambda i: (0, part)),
            ]
            + [hbm] * len(after),
            out_specs=pl.BlockSpec(stack.shape, lambda i: (0, 0, 0)),
            compiler_params=params(),
            cost_estimate=cost(3 * flops, 2 * rows * (dsl * 2 + 3 * half)),
        )(parked, acts, *after)

    theirs = lax.ppermute(grads(1, BF, in_hbm(ret)), "expert", swap)
    own = grads(0, F32)
    output_t, grad_tokens_t = pl.pallas_call(
        functools.partial(combine_kernel, experts, cap),
        out_shape=[shape((dsl, ntok), BF)] * 2,
        compiler_params=params(),
        cost_estimate=cost(6 * rows * ntok * dsl, 2 * rows * dsl * 4),
    )(ret, routes_t, weight_t)
    grad_gate, grad_up, grad_down_t = pl.pallas_call(
        add_kernel,
        out_shape=[shape((dsl, half), BF)] * 3,
        compiler_params=params(),
        cost_estimate=cost(3 * dsl * half, 24 * dsl * half),
    )(own, theirs)
    return output_t.T, grad_tokens_t.T, grad_gate, grad_up, grad_down_t.T


def solution(mesh):
    return jax.shard_map(
        per_device,
        mesh=mesh,
        in_specs=(
            P("expert", "dp"),
            P("expert", None),
            P("expert", None),
            P("dp", "expert"),
            P("dp", "expert"),
            P("expert", "dp"),
            P("expert", "dp"),
        ),
        out_specs=(
            P("expert", "dp"),
            P("expert", "dp"),
            P("dp", "expert"),
            P("dp", "expert"),
            P("expert", "dp"),
        ),
        check_vma=False,
    )
```

```python
import functools

import jax
import jax.numpy as jnp
from jax import lax
from jax.experimental import pallas as pl
from jax.experimental.pallas import tpu as pltpu
from jax.sharding import PartitionSpec as P

BF = jnp.bfloat16
F32 = jnp.float32
VMEM_BYTES = 24 * 1024 * 1024


def dot_nn(a, b):
    return lax.dot_general(a, b, (((1,), (0,)), ((), ())), preferred_element_type=F32)


def dot_nt(a, b):
    return lax.dot_general(a, b, (((1,), (1,)), ((), ())), preferred_element_type=F32)


def dot_tn(a, b):
    return lax.dot_general(a, b, (((0,), (0,)), ((), ())), preferred_element_type=F32)


def params(**more):
    return pltpu.CompilerParams(vmem_limit_bytes=VMEM_BYTES, **more)


def cost(flops, moved):
    return pl.CostEstimate(flops=flops, bytes_accessed=moved, transcendentals=0)


def pickers(routes, experts, cap):
    top, ntok = routes.shape
    names = lax.broadcasted_iota(jnp.int32, (experts, ntok), 0)
    hits = [routes[k : k + 1, :] == names for k in range(top)]
    mask = sum(jnp.where(h, 1.0, 0.0) for h in hits)
    before = lax.broadcasted_iota(jnp.int32, (ntok, ntok), 0) < lax.broadcasted_iota(
        jnp.int32, (ntok, ntok), 1
    )
    slot = dot_nn(mask.astype(BF), jnp.where(before, 1.0, 0.0).astype(BF))
    want = lax.broadcasted_iota(jnp.int32, (experts, cap, ntok), 1).astype(F32)
    picks = []
    for h in hits:
        own = jnp.where(h, slot, -1.0)
        own = jnp.broadcast_to(own[:, None, :], (experts, cap, ntok))
        pick = jnp.where(own == want, 1.0, 0.0)
        picks.append(pick.reshape(experts * cap, ntok).astype(BF))
    return picks


LANES = 128


def tiles(ref, lo, hi, cap, which):
    return jnp.concatenate(
        [
            ref[lo:hi, t * cap : (t + 1) * cap, :].reshape((hi - lo) * cap, LANES)
            for t in which
        ],
        axis=1,
    )


def put_tile(ref, lo, hi, cap, t, value):
    ref[lo:hi, t * cap : (t + 1) * cap, :] = value.reshape(hi - lo, cap, LANES)


def layout(dsl):
    full = dsl // LANES
    assert 2 * (dsl - full * LANES) == LANES
    first = [*range(full), 2 * full]
    return full * LANES, first, [*range(full, 2 * full), 2 * full]


def send_kernel(
    experts, cap, tok_hbm, cot_hbm, routes_hbm, weight_hbm, wg_hbm, wu_hbm, wd_hbm,
    out_ref, stack_hbm, tok_ref, cot_ref, routes_ref, weight_ref, zeros, sems,
):
    dsl, ntok = tok_ref.shape
    main, first, _ = layout(dsl)
    tail = dsl - main
    zeros[...] = jnp.zeros_like(zeros)
    pairs = (
        (routes_hbm, routes_ref),
        (tok_hbm, tok_ref),
        (weight_hbm, weight_ref),
        (cot_hbm, cot_ref),
        (wg_hbm, stack_hbm.at[0, pl.ds(0, dsl)]),
        (wu_hbm, stack_hbm.at[1, pl.ds(0, dsl)]),
        (wd_hbm.at[pl.ds(0, main)], stack_hbm.at[2, pl.ds(0, main)]),
        (wd_hbm.at[pl.ds(main, tail)], stack_hbm.at[2, pl.ds(dsl, tail)]),
        (zeros, stack_hbm.at[0, pl.ds(dsl, tail)]),
        (zeros, stack_hbm.at[1, pl.ds(dsl, tail)]),
        (zeros, stack_hbm.at[2, pl.ds(main, tail)]),
    )
    copies = [
        pltpu.make_async_copy(src, dst, sems.at[i])
        for i, (src, dst) in enumerate(pairs)
    ]
    for c in copies:
        c.start()
    copies[0].wait()
    picks = pickers(routes_ref[...], experts, cap)
    for c in copies[1:4]:
        c.wait()
    tok = tok_ref[...]
    cot = cot_ref[...].astype(F32)
    weight = weight_ref[...]
    rows = None
    for k, pick in enumerate(picks):
        dy = (cot * weight[k : k + 1, :]).astype(BF)
        right = jnp.concatenate([tok[:main], dy[:main], tok[main:], dy[main:]], axis=0)
        part = dot_nt(pick, right)
        rows = part if rows is None else rows + part
    rows = rows.astype(BF)
    for t in range(2 * len(first) - 1):
        put_tile(out_ref, 0, experts, cap, t, rows[:, t * LANES : (t + 1) * LANES])
    for c in copies[4:]:
        c.wait()


def terms_kernel(dsl, cap, rows_ref, own_ref, other_ref, *rest):
    sources = rows_ref.shape[0]
    outs, (held, sems) = rest[:-2], rest[-2:]
    _, first, second = layout(dsl)
    half = own_ref.shape[2]
    step = 256 // cap
    copies = []
    for lo in range(0, sources, step):
        x = tiles(rows_ref, lo, lo + step, cap, first)
        dy = tiles(rows_ref, lo, lo + step, cap, second)
        at = slice(lo * cap, (lo + step) * cap)
        for q in range(6):
            j, h = divmod(q, 2)
            w = (own_ref, other_ref)[h][j]
            left = dy if j == 2 else x
            held[at, q * half : (q + 1) * half] = dot_nn(left, w).astype(BF)
            for i in range(lo, lo + step):
                k = 6 * i + q
                copies.append(
                    pltpu.make_async_copy(
                        held.at[pl.ds(i * cap, cap), pl.ds(q * half, half)],
                        outs[k],
                        sems.at[k],
                    )
                )
                copies[-1].start()
    for c in copies:
        c.wait()


def back_kernel(dsl, cap, n, *refs):
    pieces = refs[:n]
    own_hbm, other_hbm, acts_ref, ret_hbm, held, own_ref, other_ref, ret_ref, sems = refs[n:]
    sources = n // 6
    weights = [
        [
            pltpu.make_async_copy(src.at[j], dst.at[j], sems.at[n + 3 * h + j])
            for j in range(3)
        ]
        for h, (src, dst) in enumerate(((own_hbm, own_ref), (other_hbm, other_ref)))
    ]
    half = own_ref.shape[2]
    main, _, _ = layout(dsl)
    full = main // LANES
    step = 256 // cap

    def copies(lo, h):
        for i in range(lo, lo + step):
            for q in range(h, 6, 2):
                k = 6 * i + q
                yield pltpu.make_async_copy(pieces[k], held.at[q, i], sems.at[k])

    away = []
    order = [(lo, h) for lo in range(0, sources, step) for h in range(2)]
    for lo, h in order:
        for c in copies(lo, h):
            c.start()
        if lo == 0:
            for c in weights[h]:
                c.start()
    for lo, h in order:
        for c in copies(lo, h):
            c.wait()
        hi = lo + step
        at = slice(lo * cap, hi * cap)
        gate, up, down = (
            held[2 * j + h, lo:hi].reshape(step * cap, half).astype(F32)
            for j in range(3)
        )
        sig = jax.nn.sigmoid(gate)
        active = gate * sig
        hid = (active * up).astype(BF)
        ggp = (down * up * sig * (1.0 + gate * (1.0 - sig))).astype(BF)
        gup = (down * active).astype(BF)
        for j, a in enumerate((ggp, gup, hid)):
            acts_ref[at, (3 * h + j) * half : (3 * h + j + 1) * half] = a
        if lo == 0:
            for c in weights[h]:
                c.wait()
        w_ref = (own_ref, other_ref)[h]
        part_out = dot_nt(hid, w_ref[2])
        part_back = dot_nt(ggp, w_ref[0]) + dot_nt(gup, w_ref[1])
        if h == 0:
            out, back = part_out, part_back
            continue
        out, back = out + part_out, back + part_back
        for t in range(full):
            lanes = slice(t * LANES, (t + 1) * LANES)
            put_tile(ret_ref, lo, hi, cap, t, back[:, lanes].astype(BF))
            put_tile(ret_ref, lo, hi, cap, full + t, out[:, lanes].astype(BF))
        last = back[:, main:] + out[:, main:]
        put_tile(ret_ref, lo, hi, cap, 2 * full, last.astype(BF))
        blocks = pl.ds(lo, step)
        away.append(
            pltpu.make_async_copy(
                ret_ref.at[blocks], ret_hbm.at[blocks], sems.at[n + 6 + len(away)]
            )
        )
        away[-1].start()
    for c in away:
        c.wait()


def grad_of(dsl, cap, rows_ref, acts_ref, j):
    sources = rows_ref.shape[0]
    half = acts_ref.shape[1] // 3
    main, first, second = layout(dsl)
    left = tiles(rows_ref, 0, sources, cap, second if j == 2 else first)
    grad = dot_tn(left, acts_ref[:, j * half : (j + 1) * half])
    if j == 2:
        return jnp.concatenate([grad[:main], grad[dsl:]], axis=0)
    return grad[:dsl]


def other_grads_kernel(dsl, cap, rows_ref, acts_ref, *outs):
    for j, out_ref in enumerate(outs):
        out_ref[...] = grad_of(dsl, cap, rows_ref, acts_ref, j).astype(BF)


def own_grads_kernel(dsl, cap, rows_ref, acts_ref, *rest):
    for j in range(3):
        part = grad_of(dsl, cap, rows_ref, acts_ref, j)
        rest[3 + j][...] = (part + rest[j][...].astype(F32)).astype(BF)


def combine_kernel(experts, cap, ret_ref, routes_ref, weight_ref, out_ref, grad_ref):
    dsl = out_ref.shape[0]
    main, first, _ = layout(dsl)
    tail = dsl - main
    picks = pickers(routes_ref[...], experts, cap)
    weight = weight_ref[...]
    rows = tiles(ret_ref, 0, experts, cap, range(2 * len(first) - 1))
    out = back = None
    for k, pick in enumerate(picks):
        got = dot_tn(rows, pick)
        b = jnp.concatenate([got[:main], got[2 * main : 2 * main + tail]], axis=0)
        o = jnp.concatenate([got[main : 2 * main], got[2 * main + tail :]], axis=0)
        o = o * weight[k : k + 1, :]
        out = o if out is None else out + o
        back = b if back is None else back + b
    out_ref[...] = out.astype(BF)
    grad_ref[...] = back.astype(BF)


def per_device(tokens, routes, route_weight, w_gate, w_up, w_down, cotangent):
    ntok, dsl = tokens.shape
    top = routes.shape[1]
    n_expert = lax.axis_size("expert")
    experts = n_expert // 2
    half = w_gate.shape[1]
    cap = 2 * max(1, ntok * top // experts)
    rows = experts * cap
    shape = jax.ShapeDtypeStruct
    hbm = pl.BlockSpec(memory_space=pltpu.HBM)
    vmem = pl.BlockSpec(memory_space=pltpu.VMEM)
    cores = [list(range(c, n_expert, 2)) for c in range(2)]
    swap = [(i, i ^ 1) for i in range(n_expert)]
    flops = 2 * rows * dsl * half

    def in_hbm(a):
        return pltpu.with_memory_space_constraint(a, pltpu.HBM)

    def exchange(a):
        return lax.all_to_all(a, "expert", 0, 0, axis_index_groups=cores, tiled=True)

    routes_t, weight_t = routes.T, route_weight.T
    main, first, _ = layout(dsl)
    block = shape((experts, (2 * len(first) - 1) * cap, LANES), BF)
    padded = shape((3, main + LANES, half), BF)
    stack = shape((3, dsl, half), BF)
    send, w_own = pl.pallas_call(
        functools.partial(send_kernel, experts, cap),
        out_shape=[block, padded],
        in_specs=[hbm] * 7,
        out_specs=[vmem, pl.BlockSpec(memory_space=pl.ANY)],
        scratch_shapes=[
            pltpu.VMEM((dsl, ntok), BF),
            pltpu.VMEM((dsl, ntok), BF),
            pltpu.VMEM((top, ntok), jnp.int32),
            pltpu.VMEM((top, ntok), F32),
            pltpu.VMEM((dsl - main, half), BF),
            pltpu.SemaphoreType.DMA((11,)),
        ],
        compiler_params=params(),
        cost_estimate=cost(4 * rows * ntok * dsl, 2 * rows * dsl * 4),
    )(
        *(
            in_hbm(a)
            for a in (
                tokens.T, cotangent.T, routes_t, weight_t, w_gate, w_up, w_down.T
            )
        )
    )
    got = exchange(send)
    w_other = lax.ppermute(w_own, "expert", swap)

    n = 6 * experts
    pieces = pl.pallas_call(
        functools.partial(terms_kernel, dsl, cap),
        out_shape=[pltpu.HBM((cap, half), BF)] * n,
        in_specs=[vmem] * 3,
        out_specs=[hbm] * n,
        scratch_shapes=[
            pltpu.VMEM((rows, 6 * half), BF),
            pltpu.SemaphoreType.DMA((n,)),
        ],
        compiler_params=params(),
        cost_estimate=cost(6 * flops, 2 * rows * (dsl * 2 + 6 * half)),
    )(got, w_own, w_other)
    sums = [in_hbm(a) for a in lax.psum(list(pieces), "dp")]
    acts, ret = pl.pallas_call(
        functools.partial(back_kernel, dsl, cap, n),
        out_shape=[shape((rows, 6 * half), BF), pltpu.HBM(block.shape, BF)],
        in_specs=[hbm] * (n + 2),
        out_specs=[vmem, hbm],
        scratch_shapes=[
            pltpu.VMEM((6, experts, cap, half), BF),
            pltpu.VMEM(padded.shape, BF),
            pltpu.VMEM(padded.shape, BF),
            pltpu.VMEM(block.shape, BF),
            pltpu.SemaphoreType.DMA((n + 6 + rows // 256,)),
        ],
        compiler_params=params(),
        cost_estimate=cost(6 * flops, 2 * rows * (dsl * 2 + 12 * half)),
    )(*sums, in_hbm(w_own), in_hbm(w_other))
    ret = exchange(ret)

    def grads(kernel, part, *more):
        whole = pl.BlockSpec((dsl, half), lambda i: (0, 0))
        return pl.pallas_call(
            functools.partial(kernel, dsl, cap),
            grid=(1,),
            out_shape=[shape((dsl, half), BF)] * 3,
            in_specs=[
                pl.BlockSpec(block.shape, lambda i: (0, 0, 0)),
                pl.BlockSpec((rows, 3 * half), lambda i: (0, part)),
            ]
            + [whole] * len(more),
            out_specs=[whole] * 3,
            compiler_params=params(),
            cost_estimate=cost(3 * flops, 2 * rows * (dsl * 2 + 3 * half)),
        )(got, acts, *more)

    theirs = [
        lax.ppermute(g, "expert", swap) for g in grads(other_grads_kernel, 1)
    ]
    grad_gate, grad_up, grad_down_t = grads(own_grads_kernel, 0, *theirs)
    output_t, grad_tokens_t = pl.pallas_call(
        functools.partial(combine_kernel, experts, cap),
        out_shape=[shape((dsl, ntok), BF)] * 2,
        compiler_params=params(),
        cost_estimate=cost(6 * rows * ntok * dsl, 2 * rows * dsl * 4),
    )(ret, routes_t, weight_t)
    return output_t.T, grad_tokens_t.T, grad_gate, grad_up, grad_down_t.T


def solution(mesh):
    return jax.shard_map(
        per_device,
        mesh=mesh,
        in_specs=(
            P("expert", "dp"),
            P("expert", None),
            P("expert", None),
            P("dp", "expert"),
            P("dp", "expert"),
            P("expert", "dp"),
            P("expert", "dp"),
        ),
        out_specs=(
            P("expert", "dp"),
            P("expert", "dp"),
            P("dp", "expert"),
            P("dp", "expert"),
            P("expert", "dp"),
        ),
        check_vma=False,
    )
```

```python
import functools

import jax
import jax.numpy as jnp
from jax import lax
from jax.experimental import pallas as pl
from jax.experimental.pallas import tpu as pltpu
from jax.sharding import PartitionSpec as P

BF = jnp.bfloat16
F32 = jnp.float32
VMEM_BYTES = 24 * 1024 * 1024


def dot_nn(a, b):
    return lax.dot_general(a, b, (((1,), (0,)), ((), ())), preferred_element_type=F32)


def dot_nt(a, b):
    return lax.dot_general(a, b, (((1,), (1,)), ((), ())), preferred_element_type=F32)


def dot_tn(a, b):
    return lax.dot_general(a, b, (((0,), (0,)), ((), ())), preferred_element_type=F32)


def params(**more):
    return pltpu.CompilerParams(vmem_limit_bytes=VMEM_BYTES, **more)


def cost(flops, moved):
    return pl.CostEstimate(flops=flops, bytes_accessed=moved, transcendentals=0)


def pickers(routes, experts, cap):
    top, ntok = routes.shape
    names = lax.broadcasted_iota(jnp.int32, (experts, ntok), 0)
    hits = [routes[k : k + 1, :] == names for k in range(top)]
    mask = sum(jnp.where(h, 1.0, 0.0) for h in hits)
    before = lax.broadcasted_iota(jnp.int32, (ntok, ntok), 0) < lax.broadcasted_iota(
        jnp.int32, (ntok, ntok), 1
    )
    slot = dot_nn(mask.astype(BF), jnp.where(before, 1.0, 0.0).astype(BF))
    want = lax.broadcasted_iota(jnp.int32, (experts, cap, ntok), 1).astype(F32)
    picks = []
    for h in hits:
        own = jnp.where(h, slot, -1.0)
        own = jnp.broadcast_to(own[:, None, :], (experts, cap, ntok))
        pick = jnp.where(own == want, 1.0, 0.0)
        picks.append(pick.reshape(experts * cap, ntok).astype(BF))
    return picks


LANES = 128


def tiles(ref, lo, hi, cap, which):
    return jnp.concatenate(
        [
            ref[lo:hi, t * cap : (t + 1) * cap, :].reshape((hi - lo) * cap, LANES)
            for t in which
        ],
        axis=1,
    )


def put_tile(ref, lo, hi, cap, t, value):
    ref[lo:hi, t * cap : (t + 1) * cap, :] = value.reshape(hi - lo, cap, LANES)


def layout(dsl):
    full = dsl // LANES
    assert 2 * (dsl - full * LANES) == LANES
    first = [*range(full), 2 * full]
    return full * LANES, first, [*range(full, 2 * full), 2 * full]


def send_kernel(
    experts, cap, tok_hbm, cot_hbm, routes_hbm, weight_hbm,
    out_ref, tok_ref, cot_ref, routes_ref, weight_ref, sems,
):
    dsl, ntok = tok_ref.shape
    main, first, _ = layout(dsl)
    pairs = (
        (routes_hbm, routes_ref),
        (tok_hbm, tok_ref),
        (weight_hbm, weight_ref),
        (cot_hbm, cot_ref),
    )
    copies = [
        pltpu.make_async_copy(src, dst, sems.at[i])
        for i, (src, dst) in enumerate(pairs)
    ]
    for c in copies:
        c.start()
    copies[0].wait()
    picks = pickers(routes_ref[...], experts, cap)
    for c in copies[1:]:
        c.wait()
    tok = tok_ref[...]
    cot = cot_ref[...].astype(F32)
    weight = weight_ref[...]
    rows = None
    for k, pick in enumerate(picks):
        dy = (cot * weight[k : k + 1, :]).astype(BF)
        right = jnp.concatenate([tok[:main], dy[:main], tok[main:], dy[main:]], axis=0)
        part = dot_nt(pick, right)
        rows = part if rows is None else rows + part
    rows = rows.astype(BF)
    for t in range(2 * len(first) - 1):
        put_tile(out_ref, 0, experts, cap, t, rows[:, t * LANES : (t + 1) * LANES])


def terms_kernel(cap, rows_ref, *rest):
    sources = rows_ref.shape[0]
    own_hbm, others, outs, (held, own_ref, sems) = (
        rest[:3],
        rest[3:6],
        rest[6:-3],
        rest[-3:],
    )
    dsl, half = others[0].shape
    fetches = [
        pltpu.make_async_copy(own_hbm[j], own_ref.at[j], sems.at[len(outs) + j])
        for j in range(3)
    ]
    for c in fetches:
        c.start()
    main, first, second = layout(dsl)
    gap = jnp.zeros((dsl - main, half), BF)
    step = 256 // cap
    copies = []
    for lo in range(0, sources, step):
        x = tiles(rows_ref, lo, lo + step, cap, first)
        dy = tiles(rows_ref, lo, lo + step, cap, second)
        at = slice(lo * cap, (lo + step) * cap)
        for q in (1, 3, 5, 0, 2, 4):
            j, h = divmod(q, 2)
            if lo == 0 and h == 0:
                fetches[j].wait()
            w = others[j][...] if h else own_ref[j]
            if j == 2:
                w = jnp.concatenate([w[:main], gap, w[main:]], axis=0)
            left = dy if j == 2 else x[:, :dsl]
            held[at, q * half : (q + 1) * half] = dot_nn(left, w).astype(BF)
            for i in range(lo, lo + step):
                k = 6 * i + q
                copies.append(
                    pltpu.make_async_copy(
                        held.at[pl.ds(i * cap, cap), pl.ds(q * half, half)],
                        outs[k],
                        sems.at[k],
                    )
                )
                copies[-1].start()
    for c in copies:
        c.wait()


def back_kernel(dsl, cap, n, *refs):
    pieces = refs[:n]
    acts_ref, ret_hbm, held, own_ref, other_ref, ret_ref, sems = refs[n + 6 :]
    sources = n // 6
    half = own_ref.shape[2]
    main, _, _ = layout(dsl)
    full = main // LANES
    tail = dsl - main
    step = 256 // cap
    weights = []
    for h, w_ref in enumerate((own_ref, other_ref)):
        gate, up, down = refs[n + 3 * h : n + 3 * h + 3]
        parts = (
            (gate, w_ref.at[0, pl.ds(0, dsl)]),
            (up, w_ref.at[1, pl.ds(0, dsl)]),
            (down.at[pl.ds(0, main)], w_ref.at[2, pl.ds(0, main)]),
            (down.at[pl.ds(main, tail)], w_ref.at[2, pl.ds(dsl, tail)]),
        )
        weights.append(
            [
                pltpu.make_async_copy(src, dst, sems.at[n + 4 * h + i])
                for i, (src, dst) in enumerate(parts)
            ]
        )
        for j in range(3):
            lo = main if j == 2 else dsl
            w_ref[j, lo : lo + tail] = jnp.zeros((tail, half), BF)

    def copies(lo, h):
        for i in range(lo, lo + step):
            for q in range(h, 6, 2):
                k = 6 * i + q
                yield pltpu.make_async_copy(pieces[k], held.at[q, i], sems.at[k])

    away = []
    order = [(lo, h) for lo in range(0, sources, step) for h in range(2)]
    for lo, h in order:
        for c in copies(lo, h):
            c.start()
        if lo == 0:
            for c in weights[h]:
                c.start()
    for lo, h in order:
        for c in copies(lo, h):
            c.wait()
        hi = lo + step
        at = slice(lo * cap, hi * cap)
        gate, up, down = (
            held[2 * j + h, lo:hi].reshape(step * cap, half).astype(F32)
            for j in range(3)
        )
        sig = jax.nn.sigmoid(gate)
        active = gate * sig
        hid = (active * up).astype(BF)
        ggp = (down * up * sig * (1.0 + gate * (1.0 - sig))).astype(BF)
        gup = (down * active).astype(BF)
        for j, a in enumerate((ggp, gup, hid)):
            acts_ref[at, (3 * h + j) * half : (3 * h + j + 1) * half] = a
        if lo == 0:
            for c in weights[h]:
                c.wait()
        w_ref = (own_ref, other_ref)[h]
        part_out = dot_nt(hid, w_ref[2])
        part_back = dot_nt(ggp, w_ref[0]) + dot_nt(gup, w_ref[1])
        if h == 0:
            out, back = part_out, part_back
            continue
        out, back = out + part_out, back + part_back
        for t in range(full):
            lanes = slice(t * LANES, (t + 1) * LANES)
            put_tile(ret_ref, lo, hi, cap, t, back[:, lanes].astype(BF))
            put_tile(ret_ref, lo, hi, cap, full + t, out[:, lanes].astype(BF))
        last = back[:, main:] + out[:, main:]
        put_tile(ret_ref, lo, hi, cap, 2 * full, last.astype(BF))
        blocks = pl.ds(lo, step)
        away.append(
            pltpu.make_async_copy(
                ret_ref.at[blocks], ret_hbm.at[blocks], sems.at[n + 8 + len(away)]
            )
        )
        away[-1].start()
    for c in away:
        c.wait()


def grad_of(dsl, cap, rows_ref, acts_ref, j):
    sources = rows_ref.shape[0]
    half = acts_ref.shape[1] // 3
    main, first, second = layout(dsl)
    left = tiles(rows_ref, 0, sources, cap, second if j == 2 else first)
    grad = dot_tn(left, acts_ref[:, j * half : (j + 1) * half])
    if j == 2:
        return jnp.concatenate([grad[:main], grad[dsl:]], axis=0)
    return grad[:dsl]


def other_grads_kernel(dsl, cap, rows_ref, acts_ref, *outs):
    for j, out_ref in enumerate(outs):
        out_ref[...] = grad_of(dsl, cap, rows_ref, acts_ref, j).astype(BF)


def own_grads_kernel(dsl, cap, rows_ref, acts_ref, *rest):
    for j in range(3):
        part = grad_of(dsl, cap, rows_ref, acts_ref, j)
        rest[3 + j][...] = (part + rest[j][...].astype(F32)).astype(BF)


def combine_kernel(
    experts, cap, ret_hbm, routes_ref, weight_ref, out_ref, grad_ref, ret_ref, sem
):
    fetch = pltpu.make_async_copy(ret_hbm, ret_ref, sem)
    fetch.start()
    dsl = out_ref.shape[0]
    main, first, _ = layout(dsl)
    tail = dsl - main
    picks = pickers(routes_ref[...], experts, cap)
    weight = weight_ref[...]
    fetch.wait()
    rows = tiles(ret_ref, 0, experts, cap, range(2 * len(first) - 1))
    out = back = None
    for k, pick in enumerate(picks):
        got = dot_tn(rows, pick)
        b = jnp.concatenate([got[:main], got[2 * main : 2 * main + tail]], axis=0)
        o = jnp.concatenate([got[main : 2 * main], got[2 * main + tail :]], axis=0)
        o = o * weight[k : k + 1, :]
        out = o if out is None else out + o
        back = b if back is None else back + b
    out_ref[...] = out.astype(BF)
    grad_ref[...] = back.astype(BF)


def per_device(tokens, routes, route_weight, w_gate, w_up, w_down, cotangent):
    ntok, dsl = tokens.shape
    top = routes.shape[1]
    n_expert = lax.axis_size("expert")
    experts = n_expert // 2
    half = w_gate.shape[1]
    cap = 2 * max(1, ntok * top // experts)
    rows = experts * cap
    shape = jax.ShapeDtypeStruct
    hbm = pl.BlockSpec(memory_space=pltpu.HBM)
    vmem = pl.BlockSpec(memory_space=pltpu.VMEM)
    cores = [list(range(c, n_expert, 2)) for c in range(2)]
    swap = [(i, i ^ 1) for i in range(n_expert)]
    flops = 2 * rows * dsl * half

    def in_hbm(a):
        return pltpu.with_memory_space_constraint(a, pltpu.HBM)

    def exchange(a):
        return lax.all_to_all(a, "expert", 0, 0, axis_index_groups=cores, tiled=True)

    routes_t, weight_t = routes.T, route_weight.T
    main, first, _ = layout(dsl)
    block = shape((experts, (2 * len(first) - 1) * cap, LANES), BF)
    padded = shape((3, main + LANES, half), BF)
    w_own = [w_gate, w_up, w_down.T]
    stack = shape((3, dsl, half), BF)
    send = pl.pallas_call(
        functools.partial(send_kernel, experts, cap),
        out_shape=block,
        in_specs=[hbm] * 4,
        out_specs=vmem,
        scratch_shapes=[
            pltpu.VMEM((dsl, ntok), BF),
            pltpu.VMEM((dsl, ntok), BF),
            pltpu.VMEM((top, ntok), jnp.int32),
            pltpu.VMEM((top, ntok), F32),
            pltpu.SemaphoreType.DMA((4,)),
        ],
        compiler_params=params(),
        cost_estimate=cost(4 * rows * ntok * dsl, 2 * rows * dsl * 4),
    )(*(in_hbm(a) for a in (tokens.T, cotangent.T, routes_t, weight_t)))
    got = exchange(send)
    w_other = [lax.ppermute(w, "expert", swap) for w in w_own]

    n = 6 * experts
    pieces = pl.pallas_call(
        functools.partial(terms_kernel, cap),
        out_shape=[pltpu.HBM((cap, half), BF)] * n,
        in_specs=[vmem] + [hbm] * 3 + [vmem] * 3,
        out_specs=[hbm] * n,
        scratch_shapes=[
            pltpu.VMEM((rows, 6 * half), BF),
            pltpu.VMEM(stack.shape, BF),
            pltpu.SemaphoreType.DMA((n + 3,)),
        ],
        compiler_params=params(),
        cost_estimate=cost(6 * flops, 2 * rows * (dsl * 2 + 6 * half)),
    )(got, *(in_hbm(w) for w in w_own), *w_other)
    sums = [in_hbm(a) for a in lax.psum(list(pieces), "dp")]
    acts, ret = pl.pallas_call(
        functools.partial(back_kernel, dsl, cap, n),
        out_shape=[shape((rows, 6 * half), BF), pltpu.HBM(block.shape, BF)],
        in_specs=[hbm] * (n + 6),
        out_specs=[vmem, hbm],
        scratch_shapes=[
            pltpu.VMEM((6, experts, cap, half), BF),
            pltpu.VMEM(padded.shape, BF),
            pltpu.VMEM(padded.shape, BF),
            pltpu.VMEM(block.shape, BF),
            pltpu.SemaphoreType.DMA((n + 8 + rows // 256,)),
        ],
        compiler_params=params(),
        cost_estimate=cost(6 * flops, 2 * rows * (dsl * 2 + 12 * half)),
    )(*sums, *(in_hbm(w) for w in w_own + w_other))
    ret = exchange(ret)

    def grads(kernel, part, *more):
        whole = pl.BlockSpec((dsl, half), lambda i: (0, 0))
        return pl.pallas_call(
            functools.partial(kernel, dsl, cap),
            grid=(1,),
            out_shape=[shape((dsl, half), BF)] * 3,
            in_specs=[
                pl.BlockSpec(block.shape, lambda i: (0, 0, 0)),
                pl.BlockSpec((rows, 3 * half), lambda i: (0, part)),
            ]
            + [whole] * len(more),
            out_specs=[whole] * 3,
            compiler_params=params(),
            cost_estimate=cost(3 * flops, 2 * rows * (dsl * 2 + 3 * half)),
        )(got, acts, *more)

    theirs = [
        lax.ppermute(g, "expert", swap) for g in grads(other_grads_kernel, 1)
    ]
    grad_gate, grad_up, grad_down_t = grads(own_grads_kernel, 0, *theirs)
    output_t, grad_tokens_t = pl.pallas_call(
        functools.partial(combine_kernel, experts, cap),
        out_shape=[shape((dsl, ntok), BF)] * 2,
        in_specs=[hbm, vmem, vmem],
        out_specs=[vmem] * 2,
        scratch_shapes=[pltpu.VMEM(block.shape, BF), pltpu.SemaphoreType.DMA(())],
        compiler_params=params(),
        cost_estimate=cost(6 * rows * ntok * dsl, 2 * rows * dsl * 4),
    )(in_hbm(ret), routes_t, weight_t)
    return output_t.T, grad_tokens_t.T, grad_gate, grad_up, grad_down_t.T


def solution(mesh):
    return jax.shard_map(
        per_device,
        mesh=mesh,
        in_specs=(
            P("expert", "dp"),
            P("expert", None),
            P("expert", None),
            P("dp", "expert"),
            P("dp", "expert"),
            P("expert", "dp"),
            P("expert", "dp"),
        ),
        out_specs=(
            P("expert", "dp"),
            P("expert", "dp"),
            P("dp", "expert"),
            P("dp", "expert"),
            P("expert", "dp"),
        ),
        check_vma=False,
    )
```

```python
import functools

import jax
import jax.numpy as jnp
from jax import lax
from jax.experimental import pallas as pl
from jax.experimental.pallas import tpu as pltpu
from jax.sharding import PartitionSpec as P

BF = jnp.bfloat16
F32 = jnp.float32
VMEM_BYTES = 24 * 1024 * 1024


def dot_nn(a, b):
    return lax.dot_general(a, b, (((1,), (0,)), ((), ())), preferred_element_type=F32)


def dot_nt(a, b):
    return lax.dot_general(a, b, (((1,), (1,)), ((), ())), preferred_element_type=F32)


def dot_tn(a, b):
    return lax.dot_general(a, b, (((0,), (0,)), ((), ())), preferred_element_type=F32)


def params(**more):
    return pltpu.CompilerParams(vmem_limit_bytes=VMEM_BYTES, **more)


def cost(flops, moved):
    return pl.CostEstimate(flops=flops, bytes_accessed=moved, transcendentals=0)


def pickers(routes, experts, cap):
    top, ntok = routes.shape
    names = lax.broadcasted_iota(jnp.int32, (experts, ntok), 0)
    hits = [routes[k : k + 1, :] == names for k in range(top)]
    mask = sum(jnp.where(h, 1.0, 0.0) for h in hits)
    before = lax.broadcasted_iota(jnp.int32, (ntok, ntok), 0) < lax.broadcasted_iota(
        jnp.int32, (ntok, ntok), 1
    )
    slot = dot_nn(mask.astype(BF), jnp.where(before, 1.0, 0.0).astype(BF))
    want = lax.broadcasted_iota(jnp.int32, (experts, cap, ntok), 1).astype(F32)
    picks = []
    for h in hits:
        own = jnp.where(h, slot, -1.0)
        own = jnp.broadcast_to(own[:, None, :], (experts, cap, ntok))
        pick = jnp.where(own == want, 1.0, 0.0)
        picks.append(pick.reshape(experts * cap, ntok).astype(BF))
    return picks


LANES = 128


def tiles(ref, lo, hi, cap, which):
    return jnp.concatenate(
        [
            ref[lo:hi, t * cap : (t + 1) * cap, :].reshape((hi - lo) * cap, LANES)
            for t in which
        ],
        axis=1,
    )


def put_tile(ref, lo, hi, cap, t, value):
    ref[lo:hi, t * cap : (t + 1) * cap, :] = value.reshape(hi - lo, cap, LANES)


def layout(dsl):
    full = dsl // LANES
    assert 2 * (dsl - full * LANES) == LANES
    first = [*range(full), 2 * full]
    return full * LANES, first, [*range(full, 2 * full), 2 * full]


def send_kernel(
    experts, cap, tok_hbm, cot_hbm, routes_hbm, weight_hbm,
    out_hbm, tok_ref, cot_ref, routes_ref, weight_ref, out_ref, sems,
):
    dsl, ntok = tok_ref.shape
    main, first, _ = layout(dsl)
    pairs = (
        (routes_hbm, routes_ref),
        (tok_hbm, tok_ref),
        (weight_hbm, weight_ref),
        (cot_hbm, cot_ref),
    )
    copies = [
        pltpu.make_async_copy(src, dst, sems.at[i])
        for i, (src, dst) in enumerate(pairs)
    ]
    for c in copies:
        c.start()
    copies[0].wait()
    picks = pickers(routes_ref[...], experts, cap)
    for c in copies[1:]:
        c.wait()
    tok = tok_ref[...]
    cot = cot_ref[...].astype(F32)
    weight = weight_ref[...]
    rights = []
    for k in range(2):
        dy = (cot * weight[k : k + 1, :]).astype(BF)
        rights.append(
            jnp.concatenate([tok[:main], dy[:main], tok[main:], dy[main:]], axis=0)
        )
    away = []
    step = experts // 2
    for lo in range(0, experts, step):
        hi = lo + step
        at = slice(lo * cap, hi * cap)
        rows = dot_nt(picks[0][at], rights[0]) + dot_nt(picks[1][at], rights[1])
        rows = rows.astype(BF)
        for t in range(2 * len(first) - 1):
            put_tile(out_ref, lo, hi, cap, t, rows[:, t * LANES : (t + 1) * LANES])
        blocks = pl.ds(lo, step)
        away.append(
            pltpu.make_async_copy(
                out_ref.at[blocks], out_hbm.at[blocks], sems.at[4 + len(away)]
            )
        )
        away[-1].start()
    for c in away:
        c.wait()


def fetch_kernel(*refs):
    out_ref, sems = refs[-2:]
    copies = [
        pltpu.make_async_copy(src, out_ref.at[i], sems.at[i])
        for i, src in enumerate(refs[:-2])
    ]
    for c in copies:
        c.start()
    for c in copies:
        c.wait()


def terms_kernel(cap, rows_ref, near_ref, down_hbm, *rest):
    sources = rows_ref.shape[0]
    others, outs, (held, down_ref, sems) = rest[:3], rest[3:-3], rest[-3:]
    _, dsl, half = near_ref.shape
    fetch = pltpu.make_async_copy(down_hbm, down_ref, sems.at[len(outs)])
    fetch.start()
    main, first, second = layout(dsl)
    gap = jnp.zeros((dsl - main, half), BF)
    step = 256 // cap
    copies = []
    for lo in range(0, sources, step):
        x = tiles(rows_ref, lo, lo + step, cap, first)
        dy = tiles(rows_ref, lo, lo + step, cap, second)
        at = slice(lo * cap, (lo + step) * cap)
        for q in (0, 1, 2, 3, 5, 4):
            j, h = divmod(q, 2)
            if lo == 0 and q == 4:
                fetch.wait()
            w = others[j][...] if h else down_ref[...] if j == 2 else near_ref[j]
            if j == 2:
                w = jnp.concatenate([w[:main], gap, w[main:]], axis=0)
            left = dy if j == 2 else x[:, :dsl]
            held[at, q * half : (q + 1) * half] = dot_nn(left, w).astype(BF)
            for i in range(lo, lo + step):
                k = 6 * i + q
                copies.append(
                    pltpu.make_async_copy(
                        held.at[pl.ds(i * cap, cap), pl.ds(q * half, half)],
                        outs[k],
                        sems.at[k],
                    )
                )
                copies[-1].start()
    for c in copies:
        c.wait()


def back_kernel(dsl, cap, n, *refs):
    pieces = refs[:n]
    acts_ref, ret_hbm, held, own_ref, other_ref, ret_ref, sems = refs[n + 6 :]
    sources = n // 6
    half = own_ref.shape[2]
    main, _, _ = layout(dsl)
    full = main // LANES
    tail = dsl - main
    step = 256 // cap
    weights = []
    for h, w_ref in enumerate((own_ref, other_ref)):
        gate, up, down = refs[n + 3 * h : n + 3 * h + 3]
        parts = (
            (gate, w_ref.at[0, pl.ds(0, dsl)]),
            (up, w_ref.at[1, pl.ds(0, dsl)]),
            (down.at[pl.ds(0, main)], w_ref.at[2, pl.ds(0, main)]),
            (down.at[pl.ds(main, tail)], w_ref.at[2, pl.ds(dsl, tail)]),
        )
        weights.append(
            [
                pltpu.make_async_copy(src, dst, sems.at[n + 4 * h + i])
                for i, (src, dst) in enumerate(parts)
            ]
        )
        for j in range(3):
            lo = main if j == 2 else dsl
            w_ref[j, lo : lo + tail] = jnp.zeros((tail, half), BF)

    def copies(lo, h):
        for i in range(lo, lo + step):
            for q in range(h, 6, 2):
                k = 6 * i + q
                yield pltpu.make_async_copy(pieces[k], held.at[q, i], sems.at[k])

    away = []
    order = [(lo, h) for lo in range(0, sources, step) for h in range(2)]
    for lo, h in order:
        for c in copies(lo, h):
            c.start()
        if lo == 0:
            for c in weights[h]:
                c.start()
    for lo, h in order:
        for c in copies(lo, h):
            c.wait()
        hi = lo + step
        at = slice(lo * cap, hi * cap)
        gate, up, down = (
            held[2 * j + h, lo:hi].reshape(step * cap, half).astype(F32)
            for j in range(3)
        )
        sig = jax.nn.sigmoid(gate)
        active = gate * sig
        hid = (active * up).astype(BF)
        ggp = (down * up * sig * (1.0 + gate * (1.0 - sig))).astype(BF)
        gup = (down * active).astype(BF)
        for j, a in enumerate((ggp, gup, hid)):
            acts_ref[at, (3 * h + j) * half : (3 * h + j + 1) * half] = a
        if lo == 0:
            for c in weights[h]:
                c.wait()
        w_ref = (own_ref, other_ref)[h]
        part_out = dot_nt(hid, w_ref[2])
        part_back = dot_nt(ggp, w_ref[0]) + dot_nt(gup, w_ref[1])
        if h == 0:
            out, back = part_out, part_back
            continue
        out, back = out + part_out, back + part_back
        for t in range(full):
            lanes = slice(t * LANES, (t + 1) * LANES)
            put_tile(ret_ref, lo, hi, cap, t, back[:, lanes].astype(BF))
            put_tile(ret_ref, lo, hi, cap, full + t, out[:, lanes].astype(BF))
        last = back[:, main:] + out[:, main:]
        put_tile(ret_ref, lo, hi, cap, 2 * full, last.astype(BF))
        blocks = pl.ds(lo, step)
        away.append(
            pltpu.make_async_copy(
                ret_ref.at[blocks], ret_hbm.at[blocks], sems.at[n + 8 + len(away)]
            )
        )
        away[-1].start()
    for c in away:
        c.wait()


def grad_of(dsl, cap, rows_ref, acts_ref, j):
    sources = rows_ref.shape[0]
    half = acts_ref.shape[1] // 3
    main, first, second = layout(dsl)
    left = tiles(rows_ref, 0, sources, cap, second if j == 2 else first)
    grad = dot_tn(left, acts_ref[:, j * half : (j + 1) * half])
    if j == 2:
        return jnp.concatenate([grad[:main], grad[dsl:]], axis=0)
    return grad[:dsl]


def other_grads_kernel(dsl, cap, rows_ref, acts_ref, *outs):
    for j, out_ref in enumerate(outs):
        out_ref[...] = grad_of(dsl, cap, rows_ref, acts_ref, j).astype(BF)


def own_grads_kernel(dsl, cap, rows_ref, acts_ref, *rest):
    for j in range(3):
        part = grad_of(dsl, cap, rows_ref, acts_ref, j)
        rest[3 + j][...] = (part + rest[j][...].astype(F32)).astype(BF)


def combine_kernel(
    experts, cap, ret_hbm, routes_ref, weight_ref, out_ref, grad_ref, ret_ref, sem
):
    fetch = pltpu.make_async_copy(ret_hbm, ret_ref, sem)
    fetch.start()
    dsl = out_ref.shape[0]
    main, first, _ = layout(dsl)
    tail = dsl - main
    picks = pickers(routes_ref[...], experts, cap)
    weight = weight_ref[...]
    fetch.wait()
    rows = tiles(ret_ref, 0, experts, cap, range(2 * len(first) - 1))
    out = back = None
    for k, pick in enumerate(picks):
        got = dot_tn(rows, pick)
        b = jnp.concatenate([got[:main], got[2 * main : 2 * main + tail]], axis=0)
        o = jnp.concatenate([got[main : 2 * main], got[2 * main + tail :]], axis=0)
        o = o * weight[k : k + 1, :]
        out = o if out is None else out + o
        back = b if back is None else back + b
    out_ref[...] = out.astype(BF)
    grad_ref[...] = back.astype(BF)


def per_device(tokens, routes, route_weight, w_gate, w_up, w_down, cotangent):
    ntok, dsl = tokens.shape
    top = routes.shape[1]
    n_expert = lax.axis_size("expert")
    experts = n_expert // 2
    half = w_gate.shape[1]
    cap = 2 * max(1, ntok * top // experts)
    rows = experts * cap
    shape = jax.ShapeDtypeStruct
    hbm = pl.BlockSpec(memory_space=pltpu.HBM)
    vmem = pl.BlockSpec(memory_space=pltpu.VMEM)
    cores = [list(range(c, n_expert, 2)) for c in range(2)]
    swap = [(i, i ^ 1) for i in range(n_expert)]
    flops = 2 * rows * dsl * half

    def in_hbm(a):
        return pltpu.with_memory_space_constraint(a, pltpu.HBM)

    def exchange(a):
        return lax.all_to_all(a, "expert", 0, 0, axis_index_groups=cores, tiled=True)

    routes_t, weight_t = routes.T, route_weight.T
    main, first, _ = layout(dsl)
    block = shape((experts, (2 * len(first) - 1) * cap, LANES), BF)
    padded = shape((3, main + LANES, half), BF)
    w_own = [w_gate, w_up, w_down.T]
    send = pl.pallas_call(
        functools.partial(send_kernel, experts, cap),
        out_shape=pltpu.HBM(block.shape, BF),
        in_specs=[hbm] * 4,
        out_specs=hbm,
        scratch_shapes=[
            pltpu.VMEM((dsl, ntok), BF),
            pltpu.VMEM((dsl, ntok), BF),
            pltpu.VMEM((top, ntok), jnp.int32),
            pltpu.VMEM((top, ntok), F32),
            pltpu.VMEM(block.shape, BF),
            pltpu.SemaphoreType.DMA((6,)),
        ],
        compiler_params=params(),
        cost_estimate=cost(4 * rows * ntok * dsl, 2 * rows * dsl * 4),
    )(*(in_hbm(a) for a in (tokens.T, cotangent.T, routes_t, weight_t)))
    got = exchange(send)
    w_other = [lax.ppermute(w, "expert", swap) for w in w_own]
    near = pl.pallas_call(
        fetch_kernel,
        out_shape=shape((2, dsl, half), BF),
        in_specs=[hbm] * 2,
        out_specs=vmem,
        scratch_shapes=[pltpu.SemaphoreType.DMA((2,))],
        compiler_params=params(),
        cost_estimate=cost(0, 8 * dsl * half),
    )(in_hbm(w_gate), in_hbm(w_up))

    n = 6 * experts
    pieces = pl.pallas_call(
        functools.partial(terms_kernel, cap),
        out_shape=[pltpu.HBM((cap, half), BF)] * n,
        in_specs=[vmem] * 2 + [hbm] + [vmem] * 3,
        out_specs=[hbm] * n,
        scratch_shapes=[
            pltpu.VMEM((rows, 6 * half), BF),
            pltpu.VMEM((dsl, half), BF),
            pltpu.SemaphoreType.DMA((n + 1,)),
        ],
        compiler_params=params(),
        cost_estimate=cost(6 * flops, 2 * rows * (dsl * 2 + 6 * half)),
    )(got, near, in_hbm(w_own[2]), *w_other)
    sums = [in_hbm(a) for a in lax.psum(list(pieces), "dp")]
    acts, ret = pl.pallas_call(
        functools.partial(back_kernel, dsl, cap, n),
        out_shape=[shape((rows, 6 * half), BF), pltpu.HBM(block.shape, BF)],
        in_specs=[hbm] * (n + 6),
        out_specs=[vmem, hbm],
        scratch_shapes=[
            pltpu.VMEM((6, experts, cap, half), BF),
            pltpu.VMEM(padded.shape, BF),
            pltpu.VMEM(padded.shape, BF),
            pltpu.VMEM(block.shape, BF),
            pltpu.SemaphoreType.DMA((n + 8 + rows // 256,)),
        ],
        compiler_params=params(),
        cost_estimate=cost(6 * flops, 2 * rows * (dsl * 2 + 12 * half)),
    )(*sums, *(in_hbm(w) for w in w_own + w_other))
    ret = exchange(ret)

    def grads(kernel, part, *more):
        whole = pl.BlockSpec((dsl, half), lambda i: (0, 0))
        return pl.pallas_call(
            functools.partial(kernel, dsl, cap),
            grid=(1,),
            out_shape=[shape((dsl, half), BF)] * 3,
            in_specs=[
                pl.BlockSpec(block.shape, lambda i: (0, 0, 0)),
                pl.BlockSpec((rows, 3 * half), lambda i: (0, part)),
            ]
            + [whole] * len(more),
            out_specs=[whole] * 3,
            compiler_params=params(),
            cost_estimate=cost(3 * flops, 2 * rows * (dsl * 2 + 3 * half)),
        )(got, acts, *more)

    theirs = [
        lax.ppermute(g, "expert", swap) for g in grads(other_grads_kernel, 1)
    ]
    grad_gate, grad_up, grad_down_t = grads(own_grads_kernel, 0, *theirs)
    output_t, grad_tokens_t = pl.pallas_call(
        functools.partial(combine_kernel, experts, cap),
        out_shape=[shape((dsl, ntok), BF)] * 2,
        in_specs=[hbm, vmem, vmem],
        out_specs=[vmem] * 2,
        scratch_shapes=[pltpu.VMEM(block.shape, BF), pltpu.SemaphoreType.DMA(())],
        compiler_params=params(),
        cost_estimate=cost(6 * rows * ntok * dsl, 2 * rows * dsl * 4),
    )(in_hbm(ret), routes_t, weight_t)
    return output_t.T, grad_tokens_t.T, grad_gate, grad_up, grad_down_t.T


def solution(mesh):
    return jax.shard_map(
        per_device,
        mesh=mesh,
        in_specs=(
            P("expert", "dp"),
            P("expert", None),
            P("expert", None),
            P("dp", "expert"),
            P("dp", "expert"),
            P("expert", "dp"),
            P("expert", "dp"),
        ),
        out_specs=(
            P("expert", "dp"),
            P("expert", "dp"),
            P("dp", "expert"),
            P("dp", "expert"),
            P("expert", "dp"),
        ),
        check_vma=False,
    )
```

```python
import functools

import jax
import jax.numpy as jnp
from jax import lax
from jax.experimental import pallas as pl
from jax.experimental.pallas import tpu as pltpu
from jax.sharding import PartitionSpec as P

BF = jnp.bfloat16
F32 = jnp.float32
VMEM_BYTES = 24 * 1024 * 1024


def dot_nn(a, b):
    return lax.dot_general(a, b, (((1,), (0,)), ((), ())), preferred_element_type=F32)


def dot_nt(a, b):
    return lax.dot_general(a, b, (((1,), (1,)), ((), ())), preferred_element_type=F32)


def dot_tn(a, b):
    return lax.dot_general(a, b, (((0,), (0,)), ((), ())), preferred_element_type=F32)


def params(**more):
    return pltpu.CompilerParams(vmem_limit_bytes=VMEM_BYTES, **more)


def cost(flops, moved):
    return pl.CostEstimate(flops=flops, bytes_accessed=moved, transcendentals=0)


def pickers(routes, experts, cap):
    top, ntok = routes.shape
    names = lax.broadcasted_iota(jnp.int32, (experts, ntok), 0)
    hits = [routes[k : k + 1, :] == names for k in range(top)]
    mask = sum(jnp.where(h, 1.0, 0.0) for h in hits)
    before = lax.broadcasted_iota(jnp.int32, (ntok, ntok), 0) < lax.broadcasted_iota(
        jnp.int32, (ntok, ntok), 1
    )
    slot = dot_nn(mask.astype(BF), jnp.where(before, 1.0, 0.0).astype(BF))
    want = lax.broadcasted_iota(jnp.int32, (experts, cap, ntok), 1).astype(F32)
    picks = []
    for h in hits:
        own = jnp.where(h, slot, -1.0)
        own = jnp.broadcast_to(own[:, None, :], (experts, cap, ntok))
        pick = jnp.where(own == want, 1.0, 0.0)
        picks.append(pick.reshape(experts * cap, ntok).astype(BF))
    return picks


LANES = 128


def tiles(ref, lo, hi, cap, which):
    return jnp.concatenate(
        [
            ref[lo:hi, t * cap : (t + 1) * cap, :].reshape((hi - lo) * cap, LANES)
            for t in which
        ],
        axis=1,
    )


def put_tile(ref, lo, hi, cap, t, value):
    ref[lo:hi, t * cap : (t + 1) * cap, :] = value.reshape(hi - lo, cap, LANES)


def layout(dsl):
    full = dsl // LANES
    assert 2 * (dsl - full * LANES) == LANES
    first = [*range(full), 2 * full]
    return full * LANES, first, [*range(full, 2 * full), 2 * full]


def send_kernel(
    experts, cap, tok_hbm, cot_hbm, routes_hbm, weight_hbm,
    out_hbm, tok_ref, cot_ref, routes_ref, weight_ref, out_ref, sems,
):
    dsl, ntok = tok_ref.shape
    main, first, _ = layout(dsl)
    pairs = (
        (routes_hbm, routes_ref),
        (tok_hbm, tok_ref),
        (weight_hbm, weight_ref),
        (cot_hbm, cot_ref),
    )
    copies = [
        pltpu.make_async_copy(src, dst, sems.at[i])
        for i, (src, dst) in enumerate(pairs)
    ]
    for c in copies:
        c.start()
    copies[0].wait()
    picks = pickers(routes_ref[...], experts, cap)
    for c in copies[1:]:
        c.wait()
    tok = tok_ref[...]
    cot = cot_ref[...].astype(F32)
    weight = weight_ref[...]
    rights = []
    for k in range(2):
        dy = (cot * weight[k : k + 1, :]).astype(BF)
        rights.append(
            jnp.concatenate([tok[:main], dy[:main], tok[main:], dy[main:]], axis=0)
        )
    away = []
    step = experts // 2
    for lo in range(0, experts, step):
        hi = lo + step
        at = slice(lo * cap, hi * cap)
        rows = dot_nt(picks[0][at], rights[0]) + dot_nt(picks[1][at], rights[1])
        rows = rows.astype(BF)
        for t in range(2 * len(first) - 1):
            put_tile(out_ref, lo, hi, cap, t, rows[:, t * LANES : (t + 1) * LANES])
        blocks = pl.ds(lo, step)
        away.append(
            pltpu.make_async_copy(
                out_ref.at[blocks], out_hbm.at[blocks], sems.at[4 + len(away)]
            )
        )
        away[-1].start()
    for c in away:
        c.wait()


def fetch_kernel(*refs):
    out_ref, sems = refs[-2:]
    copies = [
        pltpu.make_async_copy(src, out_ref.at[i], sems.at[i])
        for i, src in enumerate(refs[:-2])
    ]
    for c in copies:
        c.start()
    for c in copies:
        c.wait()


def terms_kernel(cap, rows_ref, near_ref, down_hbm, *rest):
    sources = rows_ref.shape[0]
    others, outs, (held, down_ref, sems) = rest[:3], rest[3:-3], rest[-3:]
    _, dsl, half = near_ref.shape
    fetch = pltpu.make_async_copy(down_hbm, down_ref, sems.at[len(outs)])
    fetch.start()
    main, first, second = layout(dsl)
    gap = jnp.zeros((dsl - main, half), BF)
    step = 256 // cap
    copies = []
    for lo in range(0, sources, step):
        x = tiles(rows_ref, lo, lo + step, cap, first)
        dy = tiles(rows_ref, lo, lo + step, cap, second)
        at = slice(lo * cap, (lo + step) * cap)
        for q in (0, 1, 2, 3, 5, 4):
            j, h = divmod(q, 2)
            if lo == 0 and q == 4:
                fetch.wait()
            w = others[j][...] if h else down_ref[...] if j == 2 else near_ref[j]
            if j == 2:
                w = jnp.concatenate([w[:main], gap, w[main:]], axis=0)
            left = dy if j == 2 else x[:, :dsl]
            held[at, q * half : (q + 1) * half] = dot_nn(left, w).astype(BF)
            for i in range(lo, lo + step):
                k = 6 * i + q
                copies.append(
                    pltpu.make_async_copy(
                        held.at[pl.ds(i * cap, cap), pl.ds(q * half, half)],
                        outs[k],
                        sems.at[k],
                    )
                )
                copies[-1].start()
    for c in copies:
        c.wait()


def back_kernel(dsl, cap, n, *refs):
    pieces = refs[:n]
    acts_ref, ret_hbm, held, own_ref, other_ref, ret_ref, sems = refs[n + 6 :]
    sources = n // 6
    half = own_ref.shape[2]
    main, _, _ = layout(dsl)
    full = main // LANES
    tail = dsl - main
    step = 256 // cap
    weights = []
    for h, w_ref in enumerate((own_ref, other_ref)):
        gate, up, down = refs[n + 3 * h : n + 3 * h + 3]
        parts = (
            (gate, w_ref.at[0, pl.ds(0, dsl)]),
            (up, w_ref.at[1, pl.ds(0, dsl)]),
            (down.at[pl.ds(0, main)], w_ref.at[2, pl.ds(0, main)]),
            (down.at[pl.ds(main, tail)], w_ref.at[2, pl.ds(dsl, tail)]),
        )
        weights.append(
            [
                pltpu.make_async_copy(src, dst, sems.at[n + 4 * h + i])
                for i, (src, dst) in enumerate(parts)
            ]
        )
        for j in range(3):
            lo = main if j == 2 else dsl
            w_ref[j, lo : lo + tail] = jnp.zeros((tail, half), BF)

    def copies(lo, h):
        for i in range(lo, lo + step):
            for q in range(h, 6, 2):
                k = 6 * i + q
                yield pltpu.make_async_copy(pieces[k], held.at[q, i], sems.at[k])

    away = []
    order = [(lo, h) for lo in range(0, sources, step) for h in range(2)]
    for lo, h in order:
        for c in copies(lo, h):
            c.start()
        if lo == 0:
            for c in weights[h]:
                c.start()
    for lo, h in order:
        for c in copies(lo, h):
            c.wait()
        hi = lo + step
        at = slice(lo * cap, hi * cap)
        gate, up, down = (
            held[2 * j + h, lo:hi].reshape(step * cap, half).astype(F32)
            for j in range(3)
        )
        sig = jax.nn.sigmoid(gate)
        active = gate * sig
        hid = (active * up).astype(BF)
        ggp = (down * up * sig * (1.0 + gate * (1.0 - sig))).astype(BF)
        gup = (down * active).astype(BF)
        for j, a in enumerate((ggp, gup, hid)):
            acts_ref[at, (3 * h + j) * half : (3 * h + j + 1) * half] = a
        if lo == 0:
            for c in weights[h]:
                c.wait()
        w_ref = (own_ref, other_ref)[h]
        part_out = dot_nt(hid, w_ref[2])
        part_back = dot_nt(ggp, w_ref[0]) + dot_nt(gup, w_ref[1])
        if h == 0:
            out, back = part_out, part_back
            continue
        out, back = out + part_out, back + part_back
        for t in range(full):
            lanes = slice(t * LANES, (t + 1) * LANES)
            put_tile(ret_ref, lo, hi, cap, t, back[:, lanes].astype(BF))
            put_tile(ret_ref, lo, hi, cap, full + t, out[:, lanes].astype(BF))
        last = back[:, main:] + out[:, main:]
        put_tile(ret_ref, lo, hi, cap, 2 * full, last.astype(BF))
        blocks = pl.ds(lo, step)
        away.append(
            pltpu.make_async_copy(
                ret_ref.at[blocks], ret_hbm.at[blocks], sems.at[n + 8 + len(away)]
            )
        )
        away[-1].start()
    for c in away:
        c.wait()


def grad_of(dsl, cap, rows_ref, acts_ref, j):
    sources = rows_ref.shape[0]
    half = acts_ref.shape[1] // 3
    main, first, second = layout(dsl)
    left = tiles(rows_ref, 0, sources, cap, second if j == 2 else first)
    grad = dot_tn(left, acts_ref[:, j * half : (j + 1) * half])
    if j == 2:
        return jnp.concatenate([grad[:main], grad[dsl:]], axis=0)
    return grad[:dsl]


def grads_kernel(dsl, cap, rows_ref, acts_ref, *outs):
    for j, out_ref in enumerate(outs):
        out_ref[...] = grad_of(dsl, cap, rows_ref, acts_ref, j).astype(out_ref.dtype)


def add_kernel(*refs):
    for j in range(3):
        refs[6 + j][...] = (refs[j][...] + refs[3 + j][...].astype(F32)).astype(BF)


def combine_kernel(
    experts, cap, ret_hbm, routes_ref, weight_ref, out_ref, grad_ref, ret_ref, sem
):
    step = experts // 4
    fetches = [
        pltpu.make_async_copy(
            ret_hbm.at[pl.ds(i * step, step)],
            ret_ref.at[pl.ds(i * step, step)],
            sem.at[i],
        )
        for i in range(4)
    ]
    for c in fetches:
        c.start()
    dsl = out_ref.shape[0]
    main, first, _ = layout(dsl)
    tail = dsl - main
    picks = pickers(routes_ref[...], experts, cap)
    weight = weight_ref[...]
    for c in fetches:
        c.wait()
    rows = tiles(ret_ref, 0, experts, cap, range(2 * len(first) - 1))
    out = back = None
    for k, pick in enumerate(picks):
        got = dot_tn(rows, pick)
        b = jnp.concatenate([got[:main], got[2 * main : 2 * main + tail]], axis=0)
        o = jnp.concatenate([got[main : 2 * main], got[2 * main + tail :]], axis=0)
        o = o * weight[k : k + 1, :]
        out = o if out is None else out + o
        back = b if back is None else back + b
    out_ref[...] = out.astype(BF)
    grad_ref[...] = back.astype(BF)


def per_device(tokens, routes, route_weight, w_gate, w_up, w_down, cotangent):
    ntok, dsl = tokens.shape
    top = routes.shape[1]
    n_expert = lax.axis_size("expert")
    experts = n_expert // 2
    half = w_gate.shape[1]
    cap = 2 * max(1, ntok * top // experts)
    rows = experts * cap
    shape = jax.ShapeDtypeStruct
    hbm = pl.BlockSpec(memory_space=pltpu.HBM)
    vmem = pl.BlockSpec(memory_space=pltpu.VMEM)
    cores = [list(range(c, n_expert, 2)) for c in range(2)]
    swap = [(i, i ^ 1) for i in range(n_expert)]
    flops = 2 * rows * dsl * half

    def in_hbm(a):
        return pltpu.with_memory_space_constraint(a, pltpu.HBM)

    def exchange(a):
        return lax.all_to_all(a, "expert", 0, 0, axis_index_groups=cores, tiled=True)

    routes_t, weight_t = routes.T, route_weight.T
    main, first, _ = layout(dsl)
    block = shape((experts, (2 * len(first) - 1) * cap, LANES), BF)
    padded = shape((3, main + LANES, half), BF)
    w_own = [w_gate, w_up, w_down.T]
    send = pl.pallas_call(
        functools.partial(send_kernel, experts, cap),
        out_shape=pltpu.HBM(block.shape, BF),
        in_specs=[hbm] * 4,
        out_specs=hbm,
        scratch_shapes=[
            pltpu.VMEM((dsl, ntok), BF),
            pltpu.VMEM((dsl, ntok), BF),
            pltpu.VMEM((top, ntok), jnp.int32),
            pltpu.VMEM((top, ntok), F32),
            pltpu.VMEM(block.shape, BF),
            pltpu.SemaphoreType.DMA((6,)),
        ],
        compiler_params=params(),
        cost_estimate=cost(4 * rows * ntok * dsl, 2 * rows * dsl * 4),
    )(*(in_hbm(a) for a in (tokens.T, cotangent.T, routes_t, weight_t)))
    got = exchange(send)
    w_other = [lax.ppermute(w, "expert", swap) for w in w_own]
    near = pl.pallas_call(
        fetch_kernel,
        out_shape=shape((2, dsl, half), BF),
        in_specs=[hbm] * 2,
        out_specs=vmem,
        scratch_shapes=[pltpu.SemaphoreType.DMA((2,))],
        compiler_params=params(),
        cost_estimate=cost(0, 8 * dsl * half),
    )(in_hbm(w_gate), in_hbm(w_up))

    n = 6 * experts
    pieces = pl.pallas_call(
        functools.partial(terms_kernel, cap),
        out_shape=[pltpu.HBM((cap, half), BF)] * n,
        in_specs=[vmem] * 2 + [hbm] + [vmem] * 3,
        out_specs=[hbm] * n,
        scratch_shapes=[
            pltpu.VMEM((rows, 6 * half), BF),
            pltpu.VMEM((dsl, half), BF),
            pltpu.SemaphoreType.DMA((n + 1,)),
        ],
        compiler_params=params(),
        cost_estimate=cost(6 * flops, 2 * rows * (dsl * 2 + 6 * half)),
    )(got, near, in_hbm(w_own[2]), *w_other)
    sums = [in_hbm(a) for a in lax.psum(list(pieces), "dp")]
    acts, ret = pl.pallas_call(
        functools.partial(back_kernel, dsl, cap, n),
        out_shape=[shape((rows, 6 * half), BF), pltpu.HBM(block.shape, BF)],
        in_specs=[hbm] * (n + 6),
        out_specs=[vmem, hbm],
        scratch_shapes=[
            pltpu.VMEM((6, experts, cap, half), BF),
            pltpu.VMEM(padded.shape, BF),
            pltpu.VMEM(padded.shape, BF),
            pltpu.VMEM(block.shape, BF),
            pltpu.SemaphoreType.DMA((n + 8 + rows // 256,)),
        ],
        compiler_params=params(),
        cost_estimate=cost(6 * flops, 2 * rows * (dsl * 2 + 12 * half)),
    )(*sums, *(in_hbm(w) for w in w_own + w_other))
    ret = exchange(ret)

    def grads(part, dtype):
        return pl.pallas_call(
            functools.partial(grads_kernel, dsl, cap),
            grid=(1,),
            out_shape=[shape((dsl, half), dtype)] * 3,
            in_specs=[
                pl.BlockSpec(block.shape, lambda i: (0, 0, 0)),
                pl.BlockSpec((rows, 3 * half), lambda i: (0, part)),
            ],
            out_specs=[pl.BlockSpec((dsl, half), lambda i: (0, 0))] * 3,
            compiler_params=params(),
            cost_estimate=cost(3 * flops, 2 * rows * (dsl * 2 + 3 * half)),
        )(got, acts)

    theirs = [lax.ppermute(g, "expert", swap) for g in grads(1, BF)]
    mine = grads(0, F32)
    grad_gate, grad_up, grad_down_t = pl.pallas_call(
        add_kernel,
        out_shape=[shape((dsl, half), BF)] * 3,
        compiler_params=params(),
        cost_estimate=cost(3 * dsl * half, 24 * dsl * half),
    )(*mine, *theirs)
    output_t, grad_tokens_t = pl.pallas_call(
        functools.partial(combine_kernel, experts, cap),
        out_shape=[shape((dsl, ntok), BF)] * 2,
        in_specs=[hbm, vmem, vmem],
        out_specs=[vmem] * 2,
        scratch_shapes=[pltpu.VMEM(block.shape, BF), pltpu.SemaphoreType.DMA((4,))],
        compiler_params=params(),
        cost_estimate=cost(6 * rows * ntok * dsl, 2 * rows * dsl * 4),
    )(in_hbm(ret), routes_t, weight_t)
    return output_t.T, grad_tokens_t.T, grad_gate, grad_up, grad_down_t.T


def solution(mesh):
    return jax.shard_map(
        per_device,
        mesh=mesh,
        in_specs=(
            P("expert", "dp"),
            P("expert", None),
            P("expert", None),
            P("dp", "expert"),
            P("dp", "expert"),
            P("expert", "dp"),
            P("expert", "dp"),
        ),
        out_specs=(
            P("expert", "dp"),
            P("expert", "dp"),
            P("dp", "expert"),
            P("dp", "expert"),
            P("expert", "dp"),
        ),
        check_vma=False,
    )
```
